128 devices in a mesh: curve: 128 (over x, y, z, core).
Axes of the slice: x: 4, y: 4, z: 4, core: 2. Of those that a mesh axis runs over, the one named last changes fastest.
Arguments:
- fields: float32 [2, 16, 16, 16, 8192], P(None, None, None, None, 'curve'), may hold values from -1 to 1
- weights: int32 [8192], P('curve'), may hold values from 1 to 24, as said below
- levels: int32 [8192], P('curve'), may hold values from 0 to 1
- neighbours: int32 [6, 8192], P(None, 'curve'), may hold values from -1 to 8191, as said below
Outputs:
- new_fields: float32 [2, 16, 16, 16, 16384], P(None, None, None, None, 'curve')
The draws below stay inside these ranges and needn't reach their ends.
Inputs may be any that keep to these rules, and one draw needn't show every extreme that they name: `weights`: under the steps' rule every block's new owner is its old owner or a rank beside it; at most 32 blocks pass between two ranks beside each other in either direction, and the blocks of every new owner have the same weight sum. `neighbours`: every entry is -1 or a block at most 16 positions away along the curve.
All inputs are finite; a program needn't handle non-finite values.
Results may differ from the reference program's by a relative error of at most 0.0003.
Values sent between devices are 32-bit elements; how exact they have to be, the bound alone decides.
A program may use at most 128 MiB of HBM per device.

```python
import jax
import jax.numpy as jnp
from jax import lax

BS = 16
BLK_DEV = 64
MOVE = 32
REACH = 16
CAP = 128
BLOCKS = 8192
N_CURVE = 128


def draw_weights(key, part):
    key_shift, key_pair, key_spot, key_total = jax.random.split(key, 4)
    small_move = MOVE // 4
    shifts = jax.random.randint(key_shift, (N_CURVE + 1,), -small_move, small_move + 1)
    spot = jax.random.randint(key_spot, (), 1, N_CURVE)
    edge_ids = jnp.arange(N_CURVE + 1)
    shifts = jnp.where(edge_ids == spot + 1, 0, shifts)
    shifts = jnp.where(edge_ids == spot, MOVE, shifts)
    shifts = jnp.where((edge_ids == 0) | (edge_ids == N_CURVE), 0, shifts)
    bounds = edge_ids * BLK_DEV + shifts
    block_ids = jnp.arange(BLOCKS)
    segment = jnp.sum((block_ids[:, None] >= bounds[None, 1:N_CURVE]).astype(jnp.int32), axis=1)
    starts = jnp.take(bounds, segment)
    lengths = jnp.take(bounds, segment + 1) - starts
    within = block_ids - starts
    target_sum = BLK_DEV * jax.random.randint(key_total, (), 7, 13)
    base_weight = target_sum // lengths
    remains = target_sum % lengths
    result = base_weight + (within < remains).astype(jnp.int32)
    jitter = jax.random.randint(key_pair, (BLOCKS,), -7, 8)
    spread = jnp.maximum(jnp.minimum(base_weight - 1, 23 - base_weight), 0)
    jitter = jnp.clip(jitter, -spread, spread)
    earlier = jnp.concatenate([jnp.zeros((1,), jitter.dtype), jitter[:-1]])
    change = jnp.where(within % 2 == 0, jnp.where(within + 1 < lengths, jitter, 0), -earlier)
    weight_out = result + change
    prev_result = jnp.concatenate([jnp.zeros((1,), result.dtype), result[:-1]])
    pair_sum = prev_result + result
    low_seg = segment == spot - 1
    high_seg = segment == spot
    weight_out = jnp.where(low_seg & (within == 0), 1, weight_out)
    weight_out = jnp.where(low_seg & (within == 1), pair_sum - 1, weight_out)
    weight_out = jnp.where(high_seg & (within == 0), 24, weight_out)
    weight_out = jnp.where(high_seg & (within == 1), pair_sum - 24, weight_out)
    return weight_out.astype(jnp.int32)


def draw_neighbours(key, part):
    key_offset, key_edge = jax.random.split(key)
    offsets = jax.random.randint(key_offset, (6, BLOCKS), -REACH, REACH + 1)
    offsets = jnp.where(offsets == 0, 1, offsets)
    block_ids = jnp.arange(BLOCKS)[None, :]
    face_ids = jnp.arange(6)[:, None]
    offsets = jnp.where((face_ids == 0) & (block_ids % 16 == 3), -REACH, offsets)
    offsets = jnp.where((face_ids == 1) & (block_ids % 16 == 5), REACH, offsets)
    target = block_ids + offsets
    boundary = jax.random.randint(key_edge, (6, BLOCKS), 0, 16) == 0
    boundary = boundary | (face_ids == 2) & (block_ids % 32 == 7)
    target = jnp.where(boundary | (target < 0) | (target >= BLOCKS), -1, target)
    return target.astype(jnp.int32)


def touch_ends(values, rng, smallest, largest):
    dims = values.shape
    index_at = [jax.random.randint(jax.random.fold_in(rng, axis), (), 0, dims[axis]) for axis in range(len(dims))]
    values = values.at[tuple(index_at)].set(smallest)
    longest = dims.index(max(dims))
    index_at[longest] = (index_at[longest] + 1) % dims[longest]
    return values.at[tuple(index_at)].set(largest)


def block_levels(key, dims, cuts, least, largest):
    factor_of = 1.0
    for dim, blocks in cuts:
        draws = jax.random.uniform(jax.random.fold_in(jax.random.fold_in(key, 6), dim), (blocks,), jnp.float32, least / len(cuts), largest / len(cuts))
        factor_of = factor_of * jnp.repeat(jnp.exp(draws), dims[dim] // blocks).reshape((-1,) + (1,) * (len(dims) - 1 - dim))
    return factor_of


def setup_inputs(seed: int = 0) -> dict:
    seeds = jax.random.split(jax.random.key(seed), 5)
    return {
        "fields": jnp.clip(jax.random.uniform(seeds[0], (2, BS, BS, BS, BLOCKS), jnp.float32, -1.0, 1.0) * block_levels(seeds[0], (2, BS, BS, BS, BLOCKS), ((4, 128),), -0.4, 0.0), -1.0, 1.0),
        "weights": draw_weights(jax.random.fold_in(seeds[4], 71), 0),
        "levels": touch_ends(jax.random.randint(seeds[2], (BLOCKS,), 0, 2), jax.random.fold_in(seeds[2], 1), 0, 1).astype(jnp.int32),
        "neighbours": draw_neighbours(jax.random.fold_in(seeds[4], 71), 0),
    }


MOBILITY_STEP = 0.0006
STIFFNESS = 1.0
COUPLING = 0.5
DIFFUSE_STEP = 0.01
SEGREGATE = 0.5


def face_table(current):
    order_field = current[0]
    surf_field = current[1]
    last_cell = order_field.shape[0] - 1
    return jnp.stack([
        jnp.stack([order_field[0], order_field[1], surf_field[0]]),
        jnp.stack([order_field[last_cell], order_field[last_cell - 1], surf_field[last_cell]]),
        jnp.stack([order_field[:, 0], order_field[:, 1], surf_field[:, 0]]),
        jnp.stack([order_field[:, last_cell], order_field[:, last_cell - 1], surf_field[:, last_cell]]),
        jnp.stack([order_field[:, :, 0], order_field[:, :, 1], surf_field[:, :, 0]]),
        jnp.stack([order_field[:, :, last_cell], order_field[:, :, last_cell - 1], surf_field[:, :, last_cell]]),
    ])


def ghosts(ext_table, lookup, neighbour_ids, own_faces):
    ghost_sets = []
    for face_idx in range(6):
        picked = jnp.take(ext_table[face_idx ^ 1], lookup[face_idx], axis=-1)
        ghost_sets.append(jnp.where(neighbour_ids[face_idx] >= 0, picked, own_faces[face_idx]))
    return ghost_sets


def framed(inner_cells, side_cells):
    edge_cells = inner_cells.shape[0]
    block_count = inner_cells.shape[-1]
    framed_cells = jnp.zeros((edge_cells + 2, edge_cells + 2, edge_cells + 2, block_count), inner_cells.dtype)
    framed_cells = framed_cells.at[1:-1, 1:-1, 1:-1].set(inner_cells)
    framed_cells = framed_cells.at[0, 1:-1, 1:-1].set(side_cells[0]).at[-1, 1:-1, 1:-1].set(side_cells[1])
    framed_cells = framed_cells.at[1:-1, 0, 1:-1].set(side_cells[2]).at[1:-1, -1, 1:-1].set(side_cells[3])
    framed_cells = framed_cells.at[1:-1, 1:-1, 0].set(side_cells[4]).at[1:-1, 1:-1, -1].set(side_cells[5])
    return framed_cells


def laplace(framed_cells, level_scale):
    centre = framed_cells[1:-1, 1:-1, 1:-1]
    beside_all = framed_cells[2:, 1:-1, 1:-1] + framed_cells[:-2, 1:-1, 1:-1]
    beside_all = beside_all + framed_cells[1:-1, 2:, 1:-1] + framed_cells[1:-1, :-2, 1:-1]
    beside_all = beside_all + framed_cells[1:-1, 1:-1, 2:] + framed_cells[1:-1, 1:-1, :-2]
    return level_scale * (beside_all - 6.0 * centre)


def slab_laplace(slab_cells, outer_layer, inner_layer, level_scale):
    padded = jnp.pad(slab_cells, ((1, 1), (1, 1), (0, 0)), mode="edge")
    tangent = padded[2:, 1:-1] + padded[:-2, 1:-1] + padded[1:-1, 2:] + padded[1:-1, :-2] - 4.0 * slab_cells
    return level_scale * (outer_layer + inner_layer - 2.0 * slab_cells + tangent)


def substep(current, ghost_sets, level_scale):
    order_field = current[0]
    surf_field = current[1]
    last_cell = order_field.shape[0] - 1
    inner_faces = [order_field[0], order_field[last_cell], order_field[:, 0], order_field[:, last_cell], order_field[:, :, 0], order_field[:, :, last_cell]]
    order_sides = [ghost_set[0] for ghost_set in ghost_sets]
    order_lap = laplace(framed(order_field, order_sides), level_scale)
    potential = order_field * order_field * order_field - order_field - STIFFNESS * order_lap - COUPLING * surf_field
    side_potential = []
    for face_idx in range(6):
        slab_cells = ghost_sets[face_idx][0]
        side_lap = slab_laplace(slab_cells, ghost_sets[face_idx][1], inner_faces[face_idx], level_scale)
        side_potential.append(slab_cells * slab_cells * slab_cells - slab_cells - STIFFNESS * side_lap - COUPLING * ghost_sets[face_idx][2])
    potential_lap = laplace(framed(potential, side_potential), level_scale)
    surf_excess = surf_field - SEGREGATE * order_field * order_field
    side_excess = [ghost_set[2] - SEGREGATE * ghost_set[0] * ghost_set[0] for ghost_set in ghost_sets]
    excess_lap = laplace(framed(surf_excess, side_excess), level_scale)
    return jnp.stack([order_field + MOBILITY_STEP * potential_lap, surf_field + DIFFUSE_STEP * excess_lap])


def advance(current, neighbours, level_scale):
    face_data = face_table(current)
    block_count = current.shape[-1]
    group_count = N_CURVE
    group_len = block_count // group_count
    lookup = jnp.clip(neighbours, 0, block_count - 1).astype(jnp.int32)
    shaped = jnp.moveaxis(current.reshape(current.shape[:-1] + (group_count, group_len)), -2, 0)
    own_groups = jnp.moveaxis(face_data.reshape(face_data.shape[:-1] + (group_count, group_len)), -2, 0)
    lookup_groups = jnp.moveaxis(lookup.reshape(6, group_count, group_len), 1, 0)
    neighbour_groups = jnp.moveaxis(neighbours.reshape(6, group_count, group_len), 1, 0)
    scale_groups = level_scale.reshape(group_count, group_len)

    def one_group(pieces):
        part_state, part_own, part_lookup, part_neighbours, part_scale = pieces
        ghost_sets = ghosts(face_data, part_lookup, part_neighbours, part_own)
        return substep(part_state, ghost_sets, part_scale)

    stepped = lax.map(one_group, (shaped, own_groups, lookup_groups, neighbour_groups, scale_groups))
    return jnp.moveaxis(stepped, 0, -2).reshape(current.shape)


def reference(fields, weights, levels, neighbours):
    block_count = weights.shape[0]
    prior_weight = (jnp.cumsum(weights) - weights).astype(jnp.int32)
    grand = jnp.sum(weights).astype(jnp.int32)
    new_owner = jnp.minimum(N_CURVE - 1, (N_CURVE * prior_weight) // grand).astype(jnp.int32)
    block_ids = jnp.arange(block_count, dtype=jnp.int32)
    new_slot = (new_owner * CAP + block_ids - new_owner * BLK_DEV + MOVE).astype(jnp.int32)
    level_scale = 1.0 + 3.0 * levels.astype(jnp.float32)
    current = fields
    for step_idx in range(2):
        current = advance(current, neighbours, level_scale)
    result = jnp.zeros((2, BS, BS, BS, N_CURVE * CAP), jnp.float32)
    return result.at[:, :, :, :, new_slot].set(current)
```

```python
import jax
import jax.numpy as jnp
from jax import lax
from jax.experimental import pallas as pl
from jax.experimental.pallas import tpu as pltpu
from jax.sharding import PartitionSpec as P

MOBILITY_STEP = 0.0006
DIFFUSE_STEP = 0.01
BS = 16
PER = 64
STAGES = ((1, 8), (8, 4), (32, 4))
PARTNERS = sum(size - 1 for _, size in STAGES)
PLANES = 2
CHUNKS = BS // PLANES
ORDER = (0, 1, 2, 3, 4, 5)
Z0 = 8
Z1 = Z0 + BS
MESH = pl.DeviceIdType.MESH
F32 = jnp.float32


def kernel(
    fields, weights, levels, nbrs, out,
    raw, wraw, lraw, nraw,
    cp, mp, ep, sf, ftz, slab, slab2, ints, kap, wown, wleft, wright, st0, st1, st2,
    spk, rpk, spk3, rpk3,
    in_sem, face_send, face_recv, move_send, move_recv, sum_send, sum_recv, w_send, w_recv,
):
    me = lax.axis_index("curve")
    count = lax.axis_size("curve")
    right = lax.rem(me + 1, count)
    left = lax.rem(me + count - 1, count)
    stage_bufs = (st0, st1, st2)

    def partner(stage, j):
        stride, size = STAGES[stage]
        digit = lax.rem(me // stride, size)
        return me + (lax.rem(digit + j, size) - digit) * stride

    loads = [
        pltpu.make_async_copy(fields.at[0], raw.at[0], in_sem.at[0]),
        pltpu.make_async_copy(fields.at[1], raw.at[1], in_sem.at[1]),
        pltpu.make_async_copy(weights, wraw, in_sem.at[2]),
        pltpu.make_async_copy(levels, lraw, in_sem.at[3]),
        pltpu.make_async_copy(nbrs, nraw, in_sem.at[4]),
    ]
    for load in loads:
        load.start()

    barrier = pltpu.get_barrier_semaphore()
    for peer in (left, right):
        pl.semaphore_signal(barrier, inc=1, device_id=(peer,), device_id_type=MESH)
    for stage, (_, size) in enumerate(STAGES):
        for j in range(1, size):
            pl.semaphore_signal(barrier, inc=1, device_id=(partner(stage, j),), device_id_type=MESH)

    lane = lax.broadcasted_iota(jnp.int32, (BS, 128), 1)
    slot16 = lane // 16
    slot32 = lane // 32

    blank = jnp.zeros((BS, 128), F32)
    for a in range(BS):
        cp[0, 1 + a, Z0:Z1] = blank
        cp[BS + 1, 1 + a, Z0:Z1] = blank
        cp[1 + a, 0, Z0:Z1] = blank
        cp[1 + a, BS + 1, Z0:Z1] = blank
        cp[1 + a, 1 : BS + 1, Z0 - 1] = blank
        cp[1 + a, 1 : BS + 1, Z1] = blank

    ints[...] = jnp.zeros((8, 128), jnp.int32)
    kap[...] = jnp.zeros((8, 128), F32)
    wown[...] = jnp.zeros((8, 128), F32)
    for load in loads[2:]:
        load.wait()
    ints[0:6, 0:PER] = nraw[...]
    kap[0:1, 0:PER] = 1.0 + 3.0 * lraw[...].astype(F32)
    wown[0:1, 0:PER] = wraw[...].astype(F32)
    kappa = jnp.broadcast_to(kap[0:1], (BS, 128))
    st0[0:1] = jnp.broadcast_to(jnp.sum(wown[0:1], axis=1, keepdims=True), (1, 128))

    loads[0].wait()

    @pl.loop(0, BS)
    def _(x):
        for y in range(BS):
            cp[x + 1, y + 1, Z0:Z1, 0:PER] = raw[0, x, y]

    loads[1].wait()

    @pl.loop(0, BS)
    def _(x):
        for y in range(BS):
            sf[x, y, :, 0:PER] = raw[1, x, y]

    pl.semaphore_wait(barrier, 2 + PARTNERS)

    copies = []

    def send(src, dst, send_sem, recv_sem, peer):
        copy = pltpu.make_async_remote_copy(
            src_ref=src, dst_ref=dst, send_sem=send_sem, recv_sem=recv_sem,
            device_id=(peer,), device_id_type=MESH,
        )
        copy.start()
        copies.append(copy)
        return copy

    def send_sums(stage):
        buf = stage_bufs[stage]
        base = sum(size - 1 for _, size in STAGES[:stage]) - 1
        return [
            send(buf.at[pl.ds(0, 1)], buf.at[pl.ds(j, 1)], sum_send.at[base + j], sum_recv.at[base + j], partner(stage, j))
            for j in range(1, STAGES[stage][1])
        ]

    def take_sums(stage, arrivals):
        for copy in arrivals:
            copy.wait_recv()
        stride, size = STAGES[stage]
        digit = lax.rem(me // stride, size)
        row = lax.broadcasted_iota(jnp.int32, (8, 128), 0)
        values = stage_bufs[stage][...]
        before = jnp.sum(jnp.where((row >= 1) & (row <= digit), values, 0.0), axis=0, keepdims=True)
        whole = jnp.sum(jnp.where(row < size, values, 0.0), axis=0, keepdims=True)
        return before, whole

    def own(f, layer, a):
        if f >= 4:
            return ftz[f - 4, layer, a]
        depth = 1 if layer == 1 else 0
        at = depth if f % 2 == 0 else BS - 1 - depth
        if f < 2:
            return sf[at, a] if layer == 2 else cp[1 + at, 1 + a, Z0:Z1]
        return sf[a, at] if layer == 2 else cp[1 + a, 1 + at, Z0:Z1]

    def draw_z():
        for a in range(BS):
            ftz[0, 0, a] = cp[1 + a, 1 : BS + 1, Z0]
            ftz[0, 1, a] = cp[1 + a, 1 : BS + 1, Z0 + 1]
            ftz[0, 2, a] = sf[a, :, 0]
            ftz[1, 0, a] = cp[1 + a, 1 : BS + 1, Z1 - 1]
            ftz[1, 1, a] = cp[1 + a, 1 : BS + 1, Z1 - 2]
            ftz[1, 2, a] = sf[a, :, BS - 1]

    def pack_face(step, f):
        for layer in range(3):
            for aa in range(2):
                to_left = to_right = None
                for j in range(8):
                    rows = own(f, layer, 2 * j + aa)
                    turned = pltpu.roll(rows, 16 * j, axis=1) if j else rows
                    to_left = turned if j == 0 else jnp.where(slot16 == j, turned, to_left)
                    to_right = turned if j == 0 else jnp.where(slot16 == (j + 3) % 8, turned, to_right)
                spk[step, 0, f, layer, aa] = to_left
                spk[step, 1, f, layer, aa] = to_right
        return [
            send(spk.at[step, d, f], rpk.at[step, d, f], face_send.at[step, d, f], face_recv.at[step, d, f], peer)
            for d, peer in ((0, left), (1, right))
        ]

    def ghost_face(step, f, arrivals):
        g = f ^ 1
        for copy in arrivals:
            copy.wait_recv()
        lookup = jnp.broadcast_to(ints[f : f + 1], (BS, 128))
        inside = lookup >= 0
        lookup = jnp.bitwise_and(lookup - me * PER, 127)
        for layer in range(3):
            for aa in range(2):
                from_right = rpk[step, 0, g, layer, aa]
                from_left = rpk[step, 1, g, layer, aa]
                for j in range(8):
                    a = 2 * j + aa
                    both = jnp.where(slot16 == (j + 3) % 8, from_left, from_right)
                    shift = (16 * (4 - j)) % 128
                    halo = pltpu.roll(both, shift, axis=1) if shift else both
                    table = jnp.where(lane < PER, own(g, layer, a), halo)
                    picked = jnp.take_along_axis(table, lookup, axis=1, mode="promise_in_bounds")
                    ghost = jnp.where(inside, picked, own(f, layer, a))
                    if layer == 0:
                        slab[f, a, Z0:Z1] = ghost
                        slab[f, a, Z0 - 1 : Z0] = ghost[0:1]
                        slab[f, a, Z1 : Z1 + 1] = ghost[BS - 1 : BS]
                    else:
                        slab2[f, layer - 1, a] = ghost
        for a in range(BS):
            g1 = slab[f, a, Z0:Z1]
            g2 = slab2[f, 0, a]
            gs = slab2[f, 1, a]
            around = slab[f, max(a - 1, 0), Z0:Z1] + slab[f, min(a + 1, BS - 1), Z0:Z1]
            around = around + slab[f, a, Z0 - 1 : Z1 - 1] + slab[f, a, Z0 + 1 : Z1 + 1]
            lap = kappa * (g2 + own(f, 0, a) + around - 6.0 * g1)
            square = g1 * g1
            mu = g1 * square - g1 - lap - 0.5 * gs
            excess = gs - 0.5 * square
            part = kappa * g1
            if f < 2:
                edge = 0 if f == 0 else BS + 1
                cell = 1 if f == 0 else BS
                mp[edge, 1 + a, Z0:Z1] = mu
                ep[edge, 1 + a, Z0:Z1] = excess
                mp[cell, 1 + a, Z0:Z1] = mp[cell, 1 + a, Z0:Z1] - part
            elif f < 4:
                edge = 0 if f == 2 else BS + 1
                cell = 1 if f == 2 else BS
                mp[1 + a, edge, Z0:Z1] = mu
                ep[1 + a, edge, Z0:Z1] = excess
                mp[1 + a, cell, Z0:Z1] = mp[1 + a, cell, Z0:Z1] - part
            else:
                edge = Z0 - 1 if f == 4 else Z1
                cell = Z0 if f == 4 else Z1 - 1
                mp[1 + a, 1 : BS + 1, edge] = mu
                ep[1 + a, 1 : BS + 1, edge] = excess
                mp[1 + a, 1 : BS + 1, cell] = mp[1 + a, 1 : BS + 1, cell] - part

    def around_of(ref, x, y):
        total = ref[x, y + 1, Z0:Z1] + ref[x + 2, y + 1, Z0:Z1]
        total = total + ref[x + 1, y, Z0:Z1] + ref[x + 1, y + 2, Z0:Z1]
        return total + ref[x + 1, y + 1, Z0 - 1 : Z1 - 1] + ref[x + 1, y + 1, Z0 + 1 : Z1 + 1]

    def potentials():
        bias = 6.0 * kappa - 1.0

        @pl.loop(0, BS)
        def _(x):
            for y in range(BS):
                c = cp[x + 1, y + 1, Z0:Z1]
                s = sf[x, y]
                square = c * c
                mp[x + 1, y + 1, Z0:Z1] = c * (square + bias) - kappa * around_of(cp, x, y) - 0.5 * s
                ep[x + 1, y + 1, Z0:Z1] = s - 0.5 * square

    c_rate = MOBILITY_STEP * kappa
    s_rate = DIFFUSE_STEP * kappa

    def next_c(x, y):
        return cp[x + 1, y + 1, Z0:Z1] + c_rate * (around_of(mp, x, y) - 6.0 * mp[x + 1, y + 1, Z0:Z1])

    def next_s(x, y):
        return sf[x, y] + s_rate * (around_of(ep, x, y) - 6.0 * ep[x + 1, y + 1, Z0:Z1])

    def exchange_faces(step):
        draw_z()
        arrivals = {f: pack_face(step, f) for f in ORDER}
        if step == 0:
            sent["w"] = [
                send(wown.at[pl.ds(0, 1)], wright.at[pl.ds(0, 1)], w_send.at[0], w_recv.at[0], left),
                send(wown.at[pl.ds(0, 1)], wleft.at[pl.ds(0, 1)], w_send.at[1], w_recv.at[1], right),
            ]
            sent["sums"] = send_sums(0)
        potentials()
        for f in ORDER:
            ghost_face(step, f ^ 1, arrivals[f])

    sent = {}
    exchange_faces(0)

    before, whole = take_sums(0, sent["sums"])
    st1[0:1] = whole
    sums1 = send_sums(1)

    @pl.loop(0, BS)
    def _(x):
        for y in range(BS):
            cp[x + 1, y + 1, Z0:Z1] = next_c(x, y)
            sf[x, y] = next_s(x, y)

    before1, whole = take_sums(1, sums1)
    st2[0:1] = whole
    sums2 = send_sums(2)
    before = before + before1

    exchange_faces(1)

    turns = (0, 64, 32, 96)
    moves = []
    for chunk in range(CHUNKS):

        @pl.loop(chunk * PLANES, (chunk + 1) * PLANES)
        def _(x):
            for comp, update in ((0, next_c), (1, next_s)):
                for yy in range(4):
                    turned = []
                    for j in range(4):
                        value = update(x, 4 * j + yy)
                        out[comp, x, 4 * j + yy] = pltpu.roll(value, 32, axis=1)
                        turned.append(pltpu.roll(value, turns[j], axis=1) if turns[j] else value)
                    u0, u1, u2, u3 = turned
                    spk3[0, x, comp, yy] = jnp.where(slot32 == 0, u0, jnp.where(slot32 == 2, u1, jnp.where(slot32 == 1, u2, u3)))
                    spk3[1, x, comp, yy] = jnp.where(slot32 == 1, u0, jnp.where(slot32 == 3, u1, jnp.where(slot32 == 2, u2, u3)))

        planes = pl.ds(chunk * PLANES, PLANES)
        moves.append([
            send(spk3.at[d, planes], rpk3.at[d, planes], move_send.at[d, chunk], move_recv.at[d, chunk], peer)
            for d, peer in ((0, left), (1, right))
        ])

    before2, total = take_sums(2, sums2)
    before = before + before2
    for copy in sent["w"]:
        copy.wait_recv()
    lane1 = lax.broadcasted_iota(jnp.int32, (8, 128), 1)
    ours = jnp.broadcast_to(wown[0:1], (8, 128))
    lefts = jnp.broadcast_to(wleft[0:1], (8, 128))
    rights = jnp.broadcast_to(wright[0:1], (8, 128))
    window = jnp.where(
        (lane1 >= 32) & (lane1 < 96),
        pltpu.roll(ours, 32, axis=1),
        pltpu.roll(jnp.where(lane1 < 32, rights, lefts), 96, axis=1),
    )
    earlier = (lax.broadcasted_iota(jnp.int32, (128, 128), 0) < lax.broadcasted_iota(jnp.int32, (128, 128), 1)).astype(F32)
    upto = jnp.dot(window, earlier, preferred_element_type=F32)
    lead = jnp.sum(jnp.where(lane1 < 32, window, 0.0), axis=1, keepdims=True)
    prior = (jnp.broadcast_to(before, (8, 128)) - lead + upto).astype(jnp.int32) * count
    whole_sum = jnp.broadcast_to(total, (8, 128)).astype(jnp.int32)
    live8 = (prior >= me * whole_sum) & (prior < (me + 1) * whole_sum)
    live = jnp.broadcast_to(live8.astype(F32)[0:1], (BS, 128)) > 0.5

    odd = jnp.bitwise_and(slot32, 1) == 1
    middle = (lane >= 32) & (lane < 96)
    for chunk in range(CHUNKS):
        for copy in moves[chunk]:
            copy.wait_recv()

        @pl.loop(chunk * PLANES, (chunk + 1) * PLANES)
        def _(x):
            for comp in range(2):
                for yy in range(4):
                    from_right = rpk3[0, x, comp, yy]
                    from_left = rpk3[1, x, comp, yy]
                    even_rows = jnp.where(odd, from_left, from_right)
                    odd_rows = jnp.where(odd, from_right, from_left)
                    halos = (
                        pltpu.roll(even_rows, 96, axis=1),
                        pltpu.roll(even_rows, 32, axis=1),
                        pltpu.roll(odd_rows, 64, axis=1),
                        odd_rows,
                    )
                    for j in range(4):
                        y = 4 * j + yy
                        out[comp, x, y] = jnp.where(live, jnp.where(middle, out[comp, x, y], halos[j]), 0.0)

    for copy in copies:
        copy.wait_send()


def body(fields, weights, levels, neighbours):
    v = pltpu.VMEM
    dma = pltpu.SemaphoreType.DMA
    hbm = pl.BlockSpec(memory_space=pltpu.HBM)
    return pl.pallas_call(
        kernel,
        out_shape=jax.ShapeDtypeStruct((2, BS, BS, BS, 2 * PER), F32),
        in_specs=[hbm] * 4,
        out_specs=pl.BlockSpec(memory_space=pltpu.VMEM),
        scratch_shapes=[
            v((2, BS, BS, BS, PER), F32),
            v((1, PER), jnp.int32),
            v((1, PER), jnp.int32),
            v((6, PER), jnp.int32),
            v((BS + 2, BS + 2, 32, 128), F32),
            v((BS + 2, BS + 2, 32, 128), F32),
            v((BS + 2, BS + 2, 32, 128), F32),
            v((BS, BS, BS, 128), F32),
            v((2, 3, BS, BS, 128), F32),
            v((6, BS, 32, 128), F32),
            v((6, 2, BS, BS, 128), F32),
            v((8, 128), jnp.int32),
            v((8, 128), F32),
            v((8, 128), F32),
            v((8, 128), F32),
            v((8, 128), F32),
            v((8, 128), F32),
            v((8, 128), F32),
            v((8, 128), F32),
            v((2, 2, 6, 3, 2, BS, 128), F32),
            v((2, 2, 6, 3, 2, BS, 128), F32),
            v((2, BS, 2, 4, BS, 128), F32),
            v((2, BS, 2, 4, BS, 128), F32),
            dma((5,)),
            dma((2, 2, 6)),
            dma((2, 2, 6)),
            dma((2, CHUNKS)),
            dma((2, CHUNKS)),
            dma((PARTNERS,)),
            dma((PARTNERS,)),
            dma((2,)),
            dma((2,)),
        ],
        compiler_params=pltpu.CompilerParams(
            collective_id=0, has_side_effects=True, vmem_limit_bytes=52 << 20
        ),
        cost_estimate=pl.CostEstimate(flops=40_000_000, bytes_accessed=8 << 20, transcendentals=0),
    )(fields, weights.reshape(1, PER), levels.reshape(1, PER), neighbours)


def solution(mesh):
    in_specs = (P(None, None, None, None, "curve"), P("curve"), P("curve"), P(None, "curve"))
    out_specs = P(None, None, None, None, "curve")
    return jax.shard_map(body, mesh=mesh, in_specs=in_specs, out_specs=out_specs, check_vma=False)
```

```python
import jax
import jax.numpy as jnp
from jax import lax
from jax.experimental import pallas as pl
from jax.experimental.pallas import tpu as pltpu
from jax.sharding import PartitionSpec as P

MOBILITY_STEP = 0.0006
DIFFUSE_STEP = 0.01
BS = 16
PER = 64
STAGES = ((1, 8), (8, 4), (32, 4))
PARTNERS = sum(size - 1 for _, size in STAGES)
LOADS = 2
PLANES = 2
CHUNKS = BS // PLANES
Z0 = 8
Z1 = Z0 + BS
MESH = pl.DeviceIdType.MESH
F32 = jnp.float32


def kernel(
    fields, weights, levels, nbrs, out,
    raw, wraw, lraw, nraw,
    cp, mp, ep, sf, ftz, turned_own, slab, slab2, ints, kap, wown, wleft, wright, st0, st1, st2,
    spk, rpk, spk3, rpk3,
    in_sem, face_send, face_recv, move_send, move_recv, sum_send, sum_recv, w_send, w_recv,
):
    me = lax.axis_index("curve")
    count = lax.axis_size("curve")
    has_left = me > 0
    has_right = me < count - 1
    left = jnp.maximum(me - 1, 0)
    right = jnp.minimum(me + 1, count - 1)
    sides = ((0, has_left, left, has_right), (1, has_right, right, has_left))
    stage_bufs = (st0, st1, st2)

    def partner(stage, j):
        stride, size = STAGES[stage]
        digit = lax.rem(me // stride, size)
        return me + (lax.rem(digit + j, size) - digit) * stride

    small = [
        pltpu.make_async_copy(weights, wraw, in_sem.at[0]),
        pltpu.make_async_copy(levels, lraw, in_sem.at[1]),
        pltpu.make_async_copy(nbrs, nraw, in_sem.at[2]),
    ]
    loads = []
    for comp in range(2):
        for part in range(LOADS):
            planes = pl.ds(part * (BS // LOADS), BS // LOADS)
            loads.append(pltpu.make_async_copy(fields.at[comp, planes], raw.at[comp, planes], in_sem.at[3 + comp * LOADS + part]))
    for load in small + loads:
        load.start()

    wleft[...] = jnp.zeros((8, 128), F32)
    wright[...] = jnp.zeros((8, 128), F32)

    barrier = pltpu.get_barrier_semaphore()
    for _, there, peer, _ in sides:

        @pl.when(there)
        def _(peer=peer):
            pl.semaphore_signal(barrier, inc=1, device_id=(peer,), device_id_type=MESH)

    for stage, (_, size) in enumerate(STAGES):
        for j in range(1, size):
            pl.semaphore_signal(barrier, inc=1, device_id=(partner(stage, j),), device_id_type=MESH)

    lane = lax.broadcasted_iota(jnp.int32, (BS, 128), 1)
    slot16 = lane // 16
    slot32 = lane // 32

    blank = jnp.zeros((BS, 128), F32)
    for a in range(BS):
        cp[0, 1 + a, Z0:Z1] = blank
        cp[BS + 1, 1 + a, Z0:Z1] = blank
        cp[1 + a, 0, Z0:Z1] = blank
        cp[1 + a, BS + 1, Z0:Z1] = blank
        cp[1 + a, 1 : BS + 1, Z0 - 1] = blank
        cp[1 + a, 1 : BS + 1, Z1] = blank

    ints[...] = jnp.zeros((8, 128), jnp.int32)
    kap[...] = jnp.zeros((8, 128), F32)
    wown[...] = jnp.zeros((8, 128), F32)
    for load in small:
        load.wait()
    ints[0:6, 0:PER] = nraw[...]
    kap[0:1, 0:PER] = 1.0 + 3.0 * lraw[...].astype(F32)
    wown[0:1, 0:PER] = wraw[...].astype(F32)
    kappa = jnp.broadcast_to(kap[0:1], (BS, 128))
    st0[0:1] = jnp.broadcast_to(jnp.sum(wown[0:1], axis=1, keepdims=True), (1, 128))

    for part in range(LOADS):
        loads[part].wait()

        @pl.loop(part * (BS // LOADS), (part + 1) * (BS // LOADS))
        def _(x):
            for y in range(BS):
                cp[x + 1, y + 1, Z0:Z1, 0:PER] = raw[0, x, y]

    for part in range(LOADS):
        loads[LOADS + part].wait()

        @pl.loop(part * (BS // LOADS), (part + 1) * (BS // LOADS))
        def _(x):
            for y in range(BS):
                sf[x, y, :, 0:PER] = raw[1, x, y]

    pl.semaphore_wait(barrier, PARTNERS + has_left.astype(jnp.int32) + has_right.astype(jnp.int32))

    copies = []
    side_copies = []

    def send(src, dst, send_sem, recv_sem, peer):
        copy = pltpu.make_async_remote_copy(
            src_ref=src, dst_ref=dst, send_sem=send_sem, recv_sem=recv_sem,
            device_id=(peer,), device_id_type=MESH,
        )
        copy.start()
        copies.append(copy)
        return copy

    def send_sides(pairs):
        arrivals = []
        for (_, there, peer, source), (src, dst, send_sem, recv_sem) in zip(sides, pairs):
            copy = pltpu.make_async_remote_copy(
                src_ref=src, dst_ref=dst, send_sem=send_sem, recv_sem=recv_sem,
                device_id=(peer,), device_id_type=MESH,
            )
            pl.when(there)(copy.start)
            side_copies.append((there, copy))
            arrivals.append((source, copy))
        return arrivals

    def take_sides(arrivals):
        for source, copy in arrivals:
            pl.when(source)(copy.wait_recv)

    def send_sums(stage):
        buf = stage_bufs[stage]
        base = sum(size - 1 for _, size in STAGES[:stage]) - 1
        return [
            send(buf.at[pl.ds(0, 1)], buf.at[pl.ds(j, 1)], sum_send.at[base + j], sum_recv.at[base + j], partner(stage, j))
            for j in range(1, STAGES[stage][1])
        ]

    def take_sums(stage, arrivals):
        for copy in arrivals:
            copy.wait_recv()
        stride, size = STAGES[stage]
        digit = lax.rem(me // stride, size)
        row = lax.broadcasted_iota(jnp.int32, (8, 128), 0)
        values = stage_bufs[stage][...]
        before = jnp.sum(jnp.where((row >= 1) & (row <= digit), values, 0.0), axis=0, keepdims=True)
        whole = jnp.sum(jnp.where(row < size, values, 0.0), axis=0, keepdims=True)
        return before, whole

    def own(f, layer, a):
        if f >= 4:
            return ftz[f - 4, layer, a]
        depth = 1 if layer == 1 else 0
        at = depth if f % 2 == 0 else BS - 1 - depth
        if f < 2:
            return sf[at, a] if layer == 2 else cp[1 + at, 1 + a, Z0:Z1]
        return sf[a, at] if layer == 2 else cp[1 + a, 1 + at, Z0:Z1]

    def draw_z():
        for a in range(BS):
            ftz[0, 0, a] = cp[1 + a, 1 : BS + 1, Z0]
            ftz[0, 1, a] = cp[1 + a, 1 : BS + 1, Z0 + 1]
            ftz[0, 2, a] = sf[a, :, 0]
            ftz[1, 0, a] = cp[1 + a, 1 : BS + 1, Z1 - 1]
            ftz[1, 1, a] = cp[1 + a, 1 : BS + 1, Z1 - 2]
            ftz[1, 2, a] = sf[a, :, BS - 1]

    def pack_pair(step, pair):
        for f in (2 * pair, 2 * pair + 1):
            for layer in range(3):
                rows = [own(f, layer, a) for a in range(BS)]
                turned = [pltpu.roll(rows[a], 16 * (a // 2), axis=1) if a >= 2 else rows[a] for a in range(BS)]
                to_left, to_right = turned[0:2], turned[0:2]
                for j in range(1, 8):
                    to_left = [jnp.where(slot16 == j, turned[2 * j + aa], to_left[aa]) for aa in range(2)]
                    to_right = [jnp.where(slot16 == (j + 3) % 8, turned[2 * j + aa], to_right[aa]) for aa in range(2)]
                to_left = [pltpu.roll(rows, 64, axis=1) for rows in to_left]
                to_right = [pltpu.roll(rows, 64, axis=1) for rows in to_right]
                for a in range(BS):
                    turned_own[f, layer, a] = turned[a]
                for aa in range(2):
                    spk[step, 0, f, layer, aa] = to_left[aa]
                    spk[step, 1, f, layer, aa] = to_right[aa]
        faces = pl.ds(2 * pair, 2)
        return send_sides([
            (spk.at[step, d, faces], rpk.at[step, d, faces], face_send.at[step, d, pair], face_recv.at[step, d, pair])
            for d in range(2)
        ])

    def ghost_face(step, f):
        g = f ^ 1
        place = jnp.broadcast_to(ints[f : f + 1], (BS, 128))
        inside = place >= 0
        place = place - me * PER
        for layer in range(3):
            from_right = [rpk[step, 0, g, layer, aa] for aa in range(2)]
            from_left = [rpk[step, 1, g, layer, aa] for aa in range(2)]
            table = []
            for a in range(BS):
                rows = jnp.where(slot16 == (a // 2 + 4) % 8, from_right[a % 2], turned_own[g, layer, a])
                table.append(jnp.where(slot16 == (a // 2 + 7) % 8, from_left[a % 2], rows))
            picked = [
                jnp.take_along_axis(table[a], jnp.bitwise_and(place + 16 * (a // 2), 127), axis=1, mode="promise_in_bounds")
                for a in range(BS)
            ]
            ghost = [jnp.where(inside, picked[a], own(f, layer, a)) for a in range(BS)]
            for a in range(BS):
                if layer == 0:
                    slab[f, a, Z0:Z1] = ghost[a]
                    slab[f, a, Z0 - 1 : Z0] = ghost[a][0:1]
                    slab[f, a, Z1 : Z1 + 1] = ghost[a][BS - 1 : BS]
                else:
                    slab2[f, layer - 1, a] = ghost[a]
        done = []
        for a in range(BS):
            g1 = slab[f, a, Z0:Z1]
            g2 = slab2[f, 0, a]
            gs = slab2[f, 1, a]
            around = slab[f, max(a - 1, 0), Z0:Z1] + slab[f, min(a + 1, BS - 1), Z0:Z1]
            around = around + slab[f, a, Z0 - 1 : Z1 - 1] + slab[f, a, Z0 + 1 : Z1 + 1]
            lap = kappa * (g2 + own(f, 0, a) + around - 6.0 * g1)
            square = g1 * g1
            mu = g1 * square - g1 - lap - 0.5 * gs
            excess = gs - 0.5 * square
            done.append((mu, excess, kappa * g1))
        for a in range(BS):
            mu, excess, part = done[a]
            if f < 2:
                edge = 0 if f == 0 else BS + 1
                cell = 1 if f == 0 else BS
                mp[edge, 1 + a, Z0:Z1] = mu
                ep[edge, 1 + a, Z0:Z1] = excess
                mp[cell, 1 + a, Z0:Z1] = mp[cell, 1 + a, Z0:Z1] - part
            elif f < 4:
                edge = 0 if f == 2 else BS + 1
                cell = 1 if f == 2 else BS
                mp[1 + a, edge, Z0:Z1] = mu
                ep[1 + a, edge, Z0:Z1] = excess
                mp[1 + a, cell, Z0:Z1] = mp[1 + a, cell, Z0:Z1] - part
            else:
                edge = Z0 - 1 if f == 4 else Z1
                cell = Z0 if f == 4 else Z1 - 1
                mp[1 + a, 1 : BS + 1, edge] = mu
                ep[1 + a, 1 : BS + 1, edge] = excess
                mp[1 + a, 1 : BS + 1, cell] = mp[1 + a, 1 : BS + 1, cell] - part

    def around_of(ref, x, y):
        total = ref[x, y + 1, Z0:Z1] + ref[x + 2, y + 1, Z0:Z1]
        total = total + ref[x + 1, y, Z0:Z1] + ref[x + 1, y + 2, Z0:Z1]
        return total + ref[x + 1, y + 1, Z0 - 1 : Z1 - 1] + ref[x + 1, y + 1, Z0 + 1 : Z1 + 1]

    def potentials():
        bias = 6.0 * kappa - 1.0

        @pl.loop(0, BS)
        def _(x):
            for y in range(BS):
                c = cp[x + 1, y + 1, Z0:Z1]
                s = sf[x, y]
                square = c * c
                mp[x + 1, y + 1, Z0:Z1] = c * (square + bias) - kappa * around_of(cp, x, y) - 0.5 * s
                ep[x + 1, y + 1, Z0:Z1] = s - 0.5 * square

    c_rate = MOBILITY_STEP * kappa
    s_rate = DIFFUSE_STEP * kappa

    def next_c(x, y):
        return cp[x + 1, y + 1, Z0:Z1] + c_rate * (around_of(mp, x, y) - 6.0 * mp[x + 1, y + 1, Z0:Z1])

    def next_s(x, y):
        return sf[x, y] + s_rate * (around_of(ep, x, y) - 6.0 * ep[x + 1, y + 1, Z0:Z1])

    def exchange_faces(step):
        draw_z()
        arrivals = [pack_pair(step, pair) for pair in range(3)]
        if step == 0:
            row = pl.ds(0, 1)
            sent["w"] = send_sides([
                (wown.at[row], wright.at[row], w_send.at[0], w_recv.at[0]),
                (wown.at[row], wleft.at[row], w_send.at[1], w_recv.at[1]),
            ])
            sent["sums"] = send_sums(0)
        potentials()
        for pair in range(3):
            take_sides(arrivals[pair])
            ghost_face(step, 2 * pair)
            ghost_face(step, 2 * pair + 1)

    sent = {}
    exchange_faces(0)

    before, whole = take_sums(0, sent["sums"])
    st1[0:1] = whole
    sums1 = send_sums(1)

    @pl.loop(0, BS)
    def _(x):
        for y in range(BS):
            cp[x + 1, y + 1, Z0:Z1] = next_c(x, y)
            sf[x, y] = next_s(x, y)

    before1, whole = take_sums(1, sums1)
    st2[0:1] = whole
    sums2 = send_sums(2)
    before = before + before1

    exchange_faces(1)

    turns = (0, 64, 32, 96)
    moves = []
    for chunk in range(CHUNKS):

        @pl.loop(chunk * PLANES, (chunk + 1) * PLANES)
        def _(x):
            for comp, update in ((0, next_c), (1, next_s)):
                for half in range(2):
                    quads = [[update(x, 4 * j + yy) for j in range(4)] for yy in (2 * half, 2 * half + 1)]
                    turned = [[pltpu.roll(q[j], turns[j], axis=1) if turns[j] else q[j] for j in range(4)] for q in quads]
                    shown = [[turned[i][2] if j == 2 else pltpu.roll(quads[i][j], 32, axis=1) for j in range(4)] for i in range(2)]
                    for i in range(2):
                        yy = 2 * half + i
                        u0, u1, u2, u3 = turned[i]
                        spk3[0, x, comp, yy] = jnp.where(slot32 == 0, u0, jnp.where(slot32 == 2, u1, jnp.where(slot32 == 1, u2, u3)))
                        spk3[1, x, comp, yy] = jnp.where(slot32 == 1, u0, jnp.where(slot32 == 3, u1, jnp.where(slot32 == 2, u2, u3)))
                        for j in range(4):
                            out[comp, x, 4 * j + yy] = shown[i][j]

        planes = pl.ds(chunk * PLANES, PLANES)
        moves.append(send_sides([
            (spk3.at[d, planes], rpk3.at[d, planes], move_send.at[d, chunk], move_recv.at[d, chunk]) for d in range(2)
        ]))

    before2, total = take_sums(2, sums2)
    before = before + before2
    take_sides(sent["w"])
    lane1 = lax.broadcasted_iota(jnp.int32, (8, 128), 1)
    ours = jnp.broadcast_to(wown[0:1], (8, 128))
    lefts = jnp.broadcast_to(wleft[0:1], (8, 128))
    rights = jnp.broadcast_to(wright[0:1], (8, 128))
    window = jnp.where(
        (lane1 >= 32) & (lane1 < 96),
        pltpu.roll(ours, 32, axis=1),
        pltpu.roll(jnp.where(lane1 < 32, rights, lefts), 96, axis=1),
    )
    earlier = (lax.broadcasted_iota(jnp.int32, (128, 128), 0) < lax.broadcasted_iota(jnp.int32, (128, 128), 1)).astype(F32)
    upto = jnp.dot(window, earlier, preferred_element_type=F32)
    lead = jnp.sum(jnp.where(lane1 < 32, window, 0.0), axis=1, keepdims=True)
    prior = (jnp.broadcast_to(before, (8, 128)) - lead + upto).astype(jnp.int32) * count
    whole_sum = jnp.broadcast_to(total, (8, 128)).astype(jnp.int32)
    live8 = (prior >= me * whole_sum) & (prior < (me + 1) * whole_sum)
    block = me * PER - 32 + lane1
    live8 = live8 & (block >= 0) & (block < count * PER)
    live = jnp.broadcast_to(live8.astype(F32)[0:1], (BS, 128)) > 0.5

    odd = jnp.bitwise_and(slot32, 1) == 1
    middle = (lane >= 32) & (lane < 96)
    for chunk in range(CHUNKS):
        take_sides(moves[chunk])

        @pl.loop(chunk * PLANES, (chunk + 1) * PLANES)
        def _(x):
            for comp in range(2):
                from_right = [rpk3[0, x, comp, yy] for yy in range(4)]
                from_left = [rpk3[1, x, comp, yy] for yy in range(4)]
                even_rows = [jnp.where(odd, from_left[yy], from_right[yy]) for yy in range(4)]
                odd_rows = [jnp.where(odd, from_right[yy], from_left[yy]) for yy in range(4)]
                halos = [
                    [pltpu.roll(rows, 96, axis=1) for rows in even_rows],
                    [pltpu.roll(rows, 32, axis=1) for rows in even_rows],
                    [pltpu.roll(rows, 64, axis=1) for rows in odd_rows],
                    odd_rows,
                ]
                merged = [jnp.where(live, jnp.where(middle, out[comp, x, y], halos[y // 4][y % 4]), 0.0) for y in range(BS)]
                for y in range(BS):
                    out[comp, x, y] = merged[y]

    for copy in copies:
        copy.wait_send()
    for there, copy in side_copies:
        pl.when(there)(copy.wait_send)


def store_kernel(window, out, sems):
    parts = 4
    copies = [
        pltpu.make_async_copy(
            window.at[k // 2, pl.ds((k % 2) * 8, 8)], out.at[k // 2, pl.ds((k % 2) * 8, 8)], sems.at[k]
        )
        for k in range(parts)
    ]
    for copy in copies:
        copy.start()
    for copy in copies:
        copy.wait()


def body(fields, weights, levels, neighbours):
    v = pltpu.VMEM
    dma = pltpu.SemaphoreType.DMA
    hbm = pl.BlockSpec(memory_space=pltpu.HBM)
    fields, weights, levels, neighbours = (
        pltpu.with_memory_space_constraint(x, pltpu.HBM)
        for x in (fields, weights.reshape(1, PER), levels.reshape(1, PER), neighbours)
    )
    window = pl.pallas_call(
        kernel,
        out_shape=pltpu.VMEM((2, BS, BS, BS, 2 * PER), F32),
        in_specs=[hbm] * 4,
        out_specs=pl.BlockSpec(memory_space=pltpu.VMEM),
        scratch_shapes=[
            v((2, BS, BS, BS, PER), F32),
            v((1, PER), jnp.int32),
            v((1, PER), jnp.int32),
            v((6, PER), jnp.int32),
            v((BS + 2, BS + 2, 32, 128), F32),
            v((BS + 2, BS + 2, 32, 128), F32),
            v((BS + 2, BS + 2, 32, 128), F32),
            v((BS, BS, BS, 128), F32),
            v((2, 3, BS, BS, 128), F32),
            v((6, 3, BS, BS, 128), F32),
            v((6, BS, 32, 128), F32),
            v((6, 2, BS, BS, 128), F32),
            v((8, 128), jnp.int32),
            v((8, 128), F32),
            v((8, 128), F32),
            v((8, 128), F32),
            v((8, 128), F32),
            v((8, 128), F32),
            v((8, 128), F32),
            v((8, 128), F32),
            v((2, 2, 6, 3, 2, BS, 128), F32),
            v((2, 2, 6, 3, 2, BS, 128), F32),
            v((2, BS, 2, 4, BS, 128), F32),
            v((2, BS, 2, 4, BS, 128), F32),
            dma((3 + 2 * LOADS,)),
            dma((2, 2, 3)),
            dma((2, 2, 3)),
            dma((2, CHUNKS)),
            dma((2, CHUNKS)),
            dma((PARTNERS,)),
            dma((PARTNERS,)),
            dma((2,)),
            dma((2,)),
        ],
        compiler_params=pltpu.CompilerParams(
            collective_id=0, has_side_effects=True, vmem_limit_bytes=44 << 20
        ),
        cost_estimate=pl.CostEstimate(flops=40_000_000, bytes_accessed=8 << 20, transcendentals=0),
    )(fields, weights, levels, neighbours)
    return pl.pallas_call(
        store_kernel,
        out_shape=jax.ShapeDtypeStruct((2, BS, BS, BS, 2 * PER), F32),
        in_specs=[pl.BlockSpec(memory_space=pltpu.VMEM)],
        out_specs=pl.BlockSpec(memory_space=pltpu.HBM),
        scratch_shapes=[dma((4,))],
        compiler_params=pltpu.CompilerParams(vmem_limit_bytes=8 << 20),
    )(pltpu.with_memory_space_constraint(window, pltpu.VMEM))


def solution(mesh):
    in_specs = (P(None, None, None, None, "curve"), P("curve"), P("curve"), P(None, "curve"))
    out_specs = P(None, None, None, None, "curve")
    return jax.shard_map(body, mesh=mesh, in_specs=in_specs, out_specs=out_specs, check_vma=False)
```

```python
import jax
import jax.numpy as jnp
from jax import lax
from jax.experimental import pallas as pl
from jax.experimental.pallas import tpu as pltpu
from jax.sharding import PartitionSpec as P

MOBILITY_STEP = 0.0006
DIFFUSE_STEP = 0.01
BS = 16
PER = 64
STAGES = ((1, 8), (8, 4), (32, 4))
PARTNERS = sum(size - 1 for _, size in STAGES)
LOADS = 2
RIM = (0, 1, BS - 2, BS - 1)
INNER = (2, BS - 2)
INNER_CHUNKS = 4
INNER_PLANES = 12 // INNER_CHUNKS
CHUNKS = INNER_CHUNKS + 3
Z0 = 8
Z1 = Z0 + BS
MESH = pl.DeviceIdType.MESH
F32 = jnp.float32


def kernel(
    fields, weights, levels, nbrs, out,
    raw, wraw, lraw, nraw,
    cp, mp, ep, sf, ftz, turned_own, slab, slab2, ints, kap, wown, wnear, st0, st1, st2,
    spk, rpk, spk_in, rpk_in, spk_mid, rpk_mid, spk_out, rpk_out,
    in_sem, face_send, face_recv, move_send, move_recv, sum_send, sum_recv, w_send, w_recv,
):
    me = lax.axis_index("curve")
    count = lax.axis_size("curve")
    first = me == 0
    last = me == count - 1
    left = jnp.where(first, 1, me - 1)
    right = jnp.where(last, count - 2, me + 1)
    spare = (me == 1) | (me == count - 2)
    sides = ((left, jnp.where(first, 2, 0)), (right, jnp.where(last, 2, 1)))
    stage_bufs = (st0, st1, st2)

    def partner(stage, j):
        stride, size = STAGES[stage]
        digit = lax.rem(me // stride, size)
        return me + (lax.rem(digit + j, size) - digit) * stride

    small = [
        pltpu.make_async_copy(weights, wraw, in_sem.at[0]),
        pltpu.make_async_copy(levels, lraw, in_sem.at[1]),
        pltpu.make_async_copy(nbrs, nraw, in_sem.at[2]),
    ]
    loads = []
    for comp in range(2):
        for part in range(LOADS):
            planes = pl.ds(part * (BS // LOADS), BS // LOADS)
            loads.append(pltpu.make_async_copy(fields.at[comp, planes], raw.at[comp, planes], in_sem.at[3 + comp * LOADS + part]))
    for load in small + loads:
        load.start()

    barrier = pltpu.get_barrier_semaphore()
    for peer in (left, right):
        pl.semaphore_signal(barrier, inc=1, device_id=(peer,), device_id_type=MESH)
    for stage, (_, size) in enumerate(STAGES):
        for j in range(1, size):
            pl.semaphore_signal(barrier, inc=1, device_id=(partner(stage, j),), device_id_type=MESH)

    lane = lax.broadcasted_iota(jnp.int32, (BS, 128), 1)
    slot16 = lane // 16
    slot32 = lane // 32

    blank = jnp.zeros((BS, 128), F32)
    for a in range(BS):
        cp[0, 1 + a, Z0:Z1] = blank
        cp[BS + 1, 1 + a, Z0:Z1] = blank
        cp[1 + a, 0, Z0:Z1] = blank
        cp[1 + a, BS + 1, Z0:Z1] = blank
        cp[1 + a, 1 : BS + 1, Z0 - 1] = blank
        cp[1 + a, 1 : BS + 1, Z1] = blank

    ints[...] = jnp.zeros((8, 128), jnp.int32)
    kap[...] = jnp.zeros((8, 128), F32)
    wown[...] = jnp.zeros((8, 128), F32)
    for load in small:
        load.wait()
    ints[0:6, 0:PER] = nraw[...]
    kap[0:1, 0:PER] = 1.0 + 3.0 * lraw[...].astype(F32)
    wown[0:1, 0:PER] = wraw[...].astype(F32)
    kappa = jnp.broadcast_to(kap[0:1], (BS, 128))
    st0[0:1] = jnp.broadcast_to(jnp.sum(wown[0:1], axis=1, keepdims=True), (1, 128))

    for part in range(LOADS):
        loads[part].wait()

        @pl.loop(part * (BS // LOADS), (part + 1) * (BS // LOADS))
        def _(x):
            for y in range(BS):
                cp[x + 1, y + 1, Z0:Z1, 0:PER] = raw[0, x, y]

    for part in range(LOADS):
        loads[LOADS + part].wait()

        @pl.loop(part * (BS // LOADS), (part + 1) * (BS // LOADS))
        def _(x):
            for y in range(BS):
                sf[x, y, :, 0:PER] = raw[1, x, y]

    pl.semaphore_wait(barrier, PARTNERS + 2 + spare.astype(jnp.int32) - (first | last).astype(jnp.int32))

    copies = []

    def send(src, dst, send_sem, recv_sem, peer):
        copy = pltpu.make_async_remote_copy(
            src_ref=src, dst_ref=dst, send_sem=send_sem, recv_sem=recv_sem,
            device_id=(peer,), device_id_type=MESH,
        )
        copy.start()
        copies.append(copy)
        return copy

    def near(kind, d, slot):
        name, *at = kind
        if name == "face":
            step, pair = at
            faces = pl.ds(2 * pair, 2)
            return spk.at[step, d, faces], rpk.at[step, slot, faces], face_send.at[step, d, pair], face_recv.at[step, slot, pair]
        if name == "weights":
            row = pl.ds(0, 1)
            return wown.at[row], wnear.at[slot, row], w_send.at[d], w_recv.at[slot]
        (chunk,) = at
        sems = move_send.at[d, chunk], move_recv.at[slot, chunk]
        if chunk < INNER_CHUNKS:
            planes = pl.ds(chunk * INNER_PLANES, INNER_PLANES)
            return spk_in.at[d, planes], rpk_in.at[slot, planes], *sems
        if chunk == INNER_CHUNKS:
            return spk_mid.at[d], rpk_mid.at[slot], *sems
        planes = pl.ds(2 * (chunk - INNER_CHUNKS - 1), 2)
        return spk_out.at[d, planes], rpk_out.at[slot, planes], *sems

    kinds = [("face", step, pair) for step in range(2) for pair in range(3)]
    kinds += [("weights",)] + [("move", chunk) for chunk in range(CHUNKS)]

    for end, slot in ((first, 1), (last, 0)):

        @pl.when(end)
        def _(slot=slot):
            for kind in kinds:
                _, place, _, sem = near(kind, 0, slot)
                pltpu.make_async_copy(near(kind, 0, 2)[1], place, sem).start()

    def send_sides(kind):
        for d, (peer, slot) in enumerate(sides):
            send(*near(kind, d, slot), peer)

    def take(kind, slot):
        src, place, send_sem, recv_sem = near(kind, 0, slot)
        pltpu.make_async_copy(place, place, recv_sem).wait()

    def take_sides(kind):
        take(kind, 0)
        take(kind, 1)

    def send_sums(stage):
        buf = stage_bufs[stage]
        base = sum(size - 1 for _, size in STAGES[:stage]) - 1
        return [
            send(buf.at[pl.ds(0, 1)], buf.at[pl.ds(j, 1)], sum_send.at[base + j], sum_recv.at[base + j], partner(stage, j))
            for j in range(1, STAGES[stage][1])
        ]

    def take_sums(stage, arrivals):
        for copy in arrivals:
            copy.wait_recv()
        stride, size = STAGES[stage]
        digit = lax.rem(me // stride, size)
        row = lax.broadcasted_iota(jnp.int32, (8, 128), 0)
        values = stage_bufs[stage][...]
        before = jnp.sum(jnp.where((row >= 1) & (row <= digit), values, 0.0), axis=0, keepdims=True)
        whole = jnp.sum(jnp.where(row < size, values, 0.0), axis=0, keepdims=True)
        return before, whole

    def own(f, layer, a):
        if f >= 4:
            return ftz[f - 4, layer, a]
        depth = 1 if layer == 1 else 0
        at = depth if f % 2 == 0 else BS - 1 - depth
        if f < 2:
            return sf[at, a] if layer == 2 else cp[1 + at, 1 + a, Z0:Z1]
        return sf[a, at] if layer == 2 else cp[1 + a, 1 + at, Z0:Z1]

    def draw_z():
        for a in range(BS):
            ftz[0, 0, a] = cp[1 + a, 1 : BS + 1, Z0]
            ftz[0, 1, a] = cp[1 + a, 1 : BS + 1, Z0 + 1]
            ftz[0, 2, a] = sf[a, :, 0]
            ftz[1, 0, a] = cp[1 + a, 1 : BS + 1, Z1 - 1]
            ftz[1, 1, a] = cp[1 + a, 1 : BS + 1, Z1 - 2]
            ftz[1, 2, a] = sf[a, :, BS - 1]

    def pack_pair(step, pair):
        for f in (2 * pair, 2 * pair + 1):
            for layer in range(3):
                rows = [own(f, layer, a) for a in range(BS)]
                turned = [pltpu.roll(rows[a], 16 * (a // 2), axis=1) if a >= 2 else rows[a] for a in range(BS)]
                to_left, to_right = turned[0:2], turned[0:2]
                for j in range(1, 8):
                    to_left = [jnp.where(slot16 == j, turned[2 * j + aa], to_left[aa]) for aa in range(2)]
                    to_right = [jnp.where(slot16 == (j + 3) % 8, turned[2 * j + aa], to_right[aa]) for aa in range(2)]
                to_left = [pltpu.roll(rows, 64, axis=1) for rows in to_left]
                to_right = [pltpu.roll(rows, 64, axis=1) for rows in to_right]
                for a in range(BS):
                    turned_own[f, layer, a] = turned[a]
                for aa in range(2):
                    spk[step, 0, f, layer, aa] = to_left[aa]
                    spk[step, 1, f, layer, aa] = to_right[aa]
        send_sides(("face", step, pair))

    def ghost_face(step, f):
        g = f ^ 1
        place = jnp.broadcast_to(ints[f : f + 1], (BS, 128))
        inside = place >= 0
        place = place - me * PER
        for layer in range(3):
            from_right = [rpk[step, 0, g, layer, aa] for aa in range(2)]
            from_left = [rpk[step, 1, g, layer, aa] for aa in range(2)]
            table = []
            for a in range(BS):
                rows = jnp.where(slot16 == (a // 2 + 4) % 8, from_right[a % 2], turned_own[g, layer, a])
                table.append(jnp.where(slot16 == (a // 2 + 7) % 8, from_left[a % 2], rows))
            picked = [
                jnp.take_along_axis(table[a], jnp.bitwise_and(place + 16 * (a // 2), 127), axis=1, mode="promise_in_bounds")
                for a in range(BS)
            ]
            ghost = [jnp.where(inside, picked[a], own(f, layer, a)) for a in range(BS)]
            for a in range(BS):
                if layer == 0:
                    slab[f, a, Z0:Z1] = ghost[a]
                    slab[f, a, Z0 - 1 : Z0] = ghost[a][0:1]
                    slab[f, a, Z1 : Z1 + 1] = ghost[a][BS - 1 : BS]
                else:
                    slab2[f, layer - 1, a] = ghost[a]
        done = []
        for a in range(BS):
            g1 = slab[f, a, Z0:Z1]
            g2 = slab2[f, 0, a]
            gs = slab2[f, 1, a]
            around = slab[f, max(a - 1, 0), Z0:Z1] + slab[f, min(a + 1, BS - 1), Z0:Z1]
            around = around + slab[f, a, Z0 - 1 : Z1 - 1] + slab[f, a, Z0 + 1 : Z1 + 1]
            lap = kappa * (g2 + own(f, 0, a) + around - 6.0 * g1)
            square = g1 * g1
            mu = g1 * square - g1 - lap - 0.5 * gs
            excess = gs - 0.5 * square
            done.append((mu, excess, kappa * g1))
        for a in range(BS):
            mu, excess, part = done[a]
            if f < 2:
                edge = 0 if f == 0 else BS + 1
                cell = 1 if f == 0 else BS
                mp[edge, 1 + a, Z0:Z1] = mu
                ep[edge, 1 + a, Z0:Z1] = excess
                mp[cell, 1 + a, Z0:Z1] = mp[cell, 1 + a, Z0:Z1] - part
            elif f < 4:
                edge = 0 if f == 2 else BS + 1
                cell = 1 if f == 2 else BS
                mp[1 + a, edge, Z0:Z1] = mu
                ep[1 + a, edge, Z0:Z1] = excess
                mp[1 + a, cell, Z0:Z1] = mp[1 + a, cell, Z0:Z1] - part
            else:
                edge = Z0 - 1 if f == 4 else Z1
                cell = Z0 if f == 4 else Z1 - 1
                mp[1 + a, 1 : BS + 1, edge] = mu
                ep[1 + a, 1 : BS + 1, edge] = excess
                mp[1 + a, 1 : BS + 1, cell] = mp[1 + a, 1 : BS + 1, cell] - part

    def around_of(ref, x, y):
        total = ref[x, y + 1, Z0:Z1] + ref[x + 2, y + 1, Z0:Z1]
        total = total + ref[x + 1, y, Z0:Z1] + ref[x + 1, y + 2, Z0:Z1]
        return total + ref[x + 1, y + 1, Z0 - 1 : Z1 - 1] + ref[x + 1, y + 1, Z0 + 1 : Z1 + 1]

    def potentials():
        bias = 6.0 * kappa - 1.0

        @pl.loop(0, BS)
        def _(x):
            for y in range(BS):
                c = cp[x + 1, y + 1, Z0:Z1]
                s = sf[x, y]
                square = c * c
                mp[x + 1, y + 1, Z0:Z1] = c * (square + bias) - kappa * around_of(cp, x, y) - 0.5 * s
                ep[x + 1, y + 1, Z0:Z1] = s - 0.5 * square

    c_rate = MOBILITY_STEP * kappa
    s_rate = DIFFUSE_STEP * kappa

    def next_c(x, y):
        return cp[x + 1, y + 1, Z0:Z1] + c_rate * (around_of(mp, x, y) - 6.0 * mp[x + 1, y + 1, Z0:Z1])

    def next_s(x, y):
        return sf[x, y] + s_rate * (around_of(ep, x, y) - 6.0 * ep[x + 1, y + 1, Z0:Z1])

    def send_faces(step):
        draw_z()
        for pair in (2, 0, 1):
            pack_pair(step, pair)

    def take_faces(step, pair):
        take_sides(("face", step, pair))
        ghost_face(step, 2 * pair)
        ghost_face(step, 2 * pair + 1)

    def renew(x, ys):
        for y in ys:
            cp[x + 1, y + 1, Z0:Z1] = next_c(x, y)
            sf[x, y] = next_s(x, y)

    send_faces(0)
    send_sides(("weights",))
    sums0 = send_sums(0)
    potentials()
    take_faces(0, 2)

    @pl.loop(*INNER)
    def _(x):
        renew(x, range(*INNER))

    before, whole = take_sums(0, sums0)
    st1[0:1] = whole
    sums1 = send_sums(1)
    take_faces(0, 0)
    take_faces(0, 1)

    @pl.loop(*INNER)
    def _(x):
        renew(x, RIM)

    for x in RIM:
        renew(x, range(BS))

    before1, whole = take_sums(1, sums1)
    st2[0:1] = whole
    sums2 = send_sums(2)
    before = before + before1

    send_faces(1)
    potentials()
    take_faces(1, 2)

    turns = (0, 64, 32, 96)

    def quad(yy):
        return RIM if yy == 3 else tuple(2 + yy + 3 * j for j in range(4))

    def evolve(x, groups, packed, plane):
        for comp, update in ((0, next_c), (1, next_s)):
            for some in (groups[:2], groups[2:]):
                quads = [[update(x, y) for y in quad(yy)] for yy in some]
                turned = [[pltpu.roll(q[j], turns[j], axis=1) if turns[j] else q[j] for j in range(4)] for q in quads]
                shown = [[turned[i][2] if j == 2 else pltpu.roll(q[j], 32, axis=1) for j in range(4)] for i, q in enumerate(quads)]
                for i, yy in enumerate(some):
                    u0, u1, u2, u3 = turned[i]
                    row = groups.index(yy)
                    packed[0, plane, comp, row] = jnp.where(slot32 == 0, u0, jnp.where(slot32 == 2, u1, jnp.where(slot32 == 1, u2, u3)))
                    packed[1, plane, comp, row] = jnp.where(slot32 == 1, u0, jnp.where(slot32 == 3, u1, jnp.where(slot32 == 2, u2, u3)))
                    for j, y in enumerate(quad(yy)):
                        out[comp, x, y] = shown[i][j]

    for chunk in range(INNER_CHUNKS):

        @pl.loop(chunk * INNER_PLANES, (chunk + 1) * INNER_PLANES)
        def _(plane):
            evolve(plane + 2, (0, 1, 2), spk_in, plane)

        send_sides(("move", chunk))

    take_faces(1, 0)
    take_faces(1, 1)

    @pl.loop(0, 12)
    def _(plane):
        evolve(plane + 2, (3,), spk_mid, plane)

    send_sides(("move", INNER_CHUNKS))
    for part in range(2):
        for k in (2 * part, 2 * part + 1):
            evolve(RIM[k], (0, 1, 2, 3), spk_out, k)
        send_sides(("move", INNER_CHUNKS + 1 + part))

    before2, total = take_sums(2, sums2)
    before = before + before2
    take_sides(("weights",))
    lane1 = lax.broadcasted_iota(jnp.int32, (8, 128), 1)
    ours = jnp.broadcast_to(wown[0:1], (8, 128))
    lefts = jnp.broadcast_to(wnear[1, 0:1], (8, 128))
    rights = jnp.broadcast_to(wnear[0, 0:1], (8, 128))
    block = me * PER - 32 + lane1
    exists = (block >= 0) & (block < count * PER)
    window = jnp.where(
        (lane1 >= 32) & (lane1 < 96),
        pltpu.roll(ours, 32, axis=1),
        pltpu.roll(jnp.where(lane1 < 32, rights, lefts), 96, axis=1),
    )
    window = jnp.where(exists, window, 0.0)
    earlier = (lax.broadcasted_iota(jnp.int32, (128, 128), 0) < lax.broadcasted_iota(jnp.int32, (128, 128), 1)).astype(F32)
    upto = jnp.dot(window, earlier, preferred_element_type=F32)
    lead = jnp.sum(jnp.where(lane1 < 32, window, 0.0), axis=1, keepdims=True)
    prior = (jnp.broadcast_to(before, (8, 128)) - lead + upto).astype(jnp.int32) * count
    whole_sum = jnp.broadcast_to(total, (8, 128)).astype(jnp.int32)
    live8 = (prior >= me * whole_sum) & (prior < (me + 1) * whole_sum)
    live8 = live8 & exists
    live = jnp.broadcast_to(live8.astype(F32)[0:1], (BS, 128)) > 0.5

    odd = jnp.bitwise_and(slot32, 1) == 1
    middle = (lane >= 32) & (lane < 96)

    def settle(x, groups, packed, plane):
        for comp in range(2):
            from_right = [packed[0, plane, comp, row] for row in range(len(groups))]
            from_left = [packed[1, plane, comp, row] for row in range(len(groups))]
            even_rows = [jnp.where(odd, a, b) for a, b in zip(from_left, from_right)]
            odd_rows = [jnp.where(odd, b, a) for a, b in zip(from_left, from_right)]
            halos = [
                [pltpu.roll(rows, 96, axis=1) for rows in even_rows],
                [pltpu.roll(rows, 32, axis=1) for rows in even_rows],
                [pltpu.roll(rows, 64, axis=1) for rows in odd_rows],
                odd_rows,
            ]
            merged = [
                (y, jnp.where(live, jnp.where(middle, out[comp, x, y], halos[j][row]), 0.0))
                for row, yy in enumerate(groups)
                for j, y in enumerate(quad(yy))
            ]
            for y, value in merged:
                out[comp, x, y] = value

    for chunk in range(INNER_CHUNKS):
        take_sides(("move", chunk))

        @pl.loop(chunk * INNER_PLANES, (chunk + 1) * INNER_PLANES)
        def _(plane):
            settle(plane + 2, (0, 1, 2), rpk_in, plane)

    take_sides(("move", INNER_CHUNKS))

    @pl.loop(0, 12)
    def _(plane):
        settle(plane + 2, (3,), rpk_mid, plane)

    for part in range(2):
        take_sides(("move", INNER_CHUNKS + 1 + part))
        for k in (2 * part, 2 * part + 1):
            settle(RIM[k], (0, 1, 2, 3), rpk_out, k)

    for copy in copies:
        copy.wait_send()

    @pl.when(spare)
    def _():
        for kind in kinds:
            take(kind, 2)


def store_kernel(window, out, sems):
    parts = 4
    copies = [
        pltpu.make_async_copy(
            window.at[k // 2, pl.ds((k % 2) * 8, 8)], out.at[k // 2, pl.ds((k % 2) * 8, 8)], sems.at[k]
        )
        for k in range(parts)
    ]
    for copy in copies:
        copy.start()
    for copy in copies:
        copy.wait()


def body(fields, weights, levels, neighbours):
    v = pltpu.VMEM
    dma = pltpu.SemaphoreType.DMA
    hbm = pl.BlockSpec(memory_space=pltpu.HBM)
    fields, weights, levels, neighbours = (
        pltpu.with_memory_space_constraint(x, pltpu.HBM)
        for x in (fields, weights.reshape(1, PER), levels.reshape(1, PER), neighbours)
    )
    window = pl.pallas_call(
        kernel,
        out_shape=pltpu.VMEM((2, BS, BS, BS, 2 * PER), F32),
        in_specs=[hbm] * 4,
        out_specs=pl.BlockSpec(memory_space=pltpu.VMEM),
        scratch_shapes=[
            v((2, BS, BS, BS, PER), F32),
            v((1, PER), jnp.int32),
            v((1, PER), jnp.int32),
            v((6, PER), jnp.int32),
            v((BS + 2, BS + 2, 32, 128), F32),
            v((BS + 2, BS + 2, 32, 128), F32),
            v((BS + 2, BS + 2, 32, 128), F32),
            v((BS, BS, BS, 128), F32),
            v((2, 3, BS, BS, 128), F32),
            v((6, 3, BS, BS, 128), F32),
            v((6, BS, 32, 128), F32),
            v((6, 2, BS, BS, 128), F32),
            v((8, 128), jnp.int32),
            v((8, 128), F32),
            v((8, 128), F32),
            v((3, 8, 128), F32),
            v((8, 128), F32),
            v((8, 128), F32),
            v((8, 128), F32),
            v((2, 2, 6, 3, 2, BS, 128), F32),
            v((2, 3, 6, 3, 2, BS, 128), F32),
            v((2, 12, 2, 3, BS, 128), F32),
            v((3, 12, 2, 3, BS, 128), F32),
            v((2, 12, 2, 1, BS, 128), F32),
            v((3, 12, 2, 1, BS, 128), F32),
            v((2, 4, 2, 4, BS, 128), F32),
            v((3, 4, 2, 4, BS, 128), F32),
            dma((3 + 2 * LOADS,)),
            dma((2, 2, 3)),
            dma((2, 3, 3)),
            dma((2, CHUNKS)),
            dma((3, CHUNKS)),
            dma((PARTNERS,)),
            dma((PARTNERS,)),
            dma((2,)),
            dma((3,)),
        ],
        compiler_params=pltpu.CompilerParams(
            collective_id=0, has_side_effects=True, vmem_limit_bytes=44 << 20
        ),
        cost_estimate=pl.CostEstimate(flops=40_000_000, bytes_accessed=8 << 20, transcendentals=0),
    )(fields, weights, levels, neighbours)
    return pl.pallas_call(
        store_kernel,
        out_shape=jax.ShapeDtypeStruct((2, BS, BS, BS, 2 * PER), F32),
        in_specs=[pl.BlockSpec(memory_space=pltpu.VMEM)],
        out_specs=pl.BlockSpec(memory_space=pltpu.HBM),
        scratch_shapes=[dma((4,))],
        compiler_params=pltpu.CompilerParams(vmem_limit_bytes=8 << 20),
    )(pltpu.with_memory_space_constraint(window, pltpu.VMEM))


def solution(mesh):
    in_specs = (P(None, None, None, None, "curve"), P("curve"), P("curve"), P(None, "curve"))
    out_specs = P(None, None, None, None, "curve")
    return jax.shard_map(body, mesh=mesh, in_specs=in_specs, out_specs=out_specs, check_vma=False)
```

```python
import jax
import jax.numpy as jnp
from jax import lax
from jax.experimental import pallas as pl
from jax.experimental.pallas import tpu as pltpu
from jax.sharding import PartitionSpec as P

MOBILITY_STEP = 0.0006
DIFFUSE_STEP = 0.01
BS = 16
PER = 64
STAGES = ((1, 8), (8, 4), (32, 4))
PARTNERS = sum(size - 1 for _, size in STAGES)
LOADS = 2
RIM = (0, 1, BS - 2, BS - 1)
INNER = (2, BS - 2)
INNER_CUTS = (0, 1, 4, 8, 12)
INNER_CHUNKS = len(INNER_CUTS) - 1
CHUNKS = INNER_CHUNKS + 3
Z0 = 8
Z1 = Z0 + BS
MESH = pl.DeviceIdType.MESH
F32 = jnp.float32


def kernel(
    fields, weights, levels, nbrs, out,
    raw, wraw, lraw, nraw,
    cp, mp, ep, sf, ftz, turned_own, slab, slab2, ints, kap, wown, wnear, st0, st1, st2,
    spk, rpk, spk_in, rpk_in, spk_mid, rpk_mid, spk_out, rpk_out,
    in_sem, face_send, face_recv, move_send, move_recv, sum_send, sum_recv, w_send, w_recv,
):
    me = lax.axis_index("curve")
    count = lax.axis_size("curve")
    first = me == 0
    last = me == count - 1
    left = jnp.where(first, 1, me - 1)
    right = jnp.where(last, count - 2, me + 1)
    spare = (me == 1) | (me == count - 2)
    sides = ((left, jnp.where(first, 2, 0)), (right, jnp.where(last, 2, 1)))
    stage_bufs = (st0, st1, st2)

    def partner(stage, j):
        stride, size = STAGES[stage]
        digit = lax.rem(me // stride, size)
        return me + (lax.rem(digit + j, size) - digit) * stride

    small = [
        pltpu.make_async_copy(weights, wraw, in_sem.at[0]),
        pltpu.make_async_copy(levels, lraw, in_sem.at[1]),
        pltpu.make_async_copy(nbrs, nraw, in_sem.at[2]),
    ]
    loads = []
    for comp in range(2):
        for part in range(LOADS):
            planes = pl.ds(part * (BS // LOADS), BS // LOADS)
            loads.append(pltpu.make_async_copy(fields.at[comp, planes], raw.at[comp, planes], in_sem.at[3 + comp * LOADS + part]))
    for load in small + loads:
        load.start()

    barrier = pltpu.get_barrier_semaphore()
    for peer in (left, right):
        pl.semaphore_signal(barrier, inc=1, device_id=(peer,), device_id_type=MESH)
    for stage, (_, size) in enumerate(STAGES):
        for j in range(1, size):
            pl.semaphore_signal(barrier, inc=1, device_id=(partner(stage, j),), device_id_type=MESH)

    lane = lax.broadcasted_iota(jnp.int32, (BS, 128), 1)
    slot16 = lane // 16
    slot32 = lane // 32

    blank = jnp.zeros((BS, 128), F32)
    for a in range(BS):
        cp[0, 1 + a, Z0:Z1] = blank
        cp[BS + 1, 1 + a, Z0:Z1] = blank
        cp[1 + a, 0, Z0:Z1] = blank
        cp[1 + a, BS + 1, Z0:Z1] = blank
        cp[1 + a, 1 : BS + 1, Z0 - 1] = blank
        cp[1 + a, 1 : BS + 1, Z1] = blank

    ints[...] = jnp.zeros((8, 128), jnp.int32)
    kap[...] = jnp.zeros((8, 128), F32)
    wown[...] = jnp.zeros((8, 128), F32)
    for load in small:
        load.wait()
    ints[0:6, 0:PER] = nraw[...]
    kap[0:1, 0:PER] = 1.0 + 3.0 * lraw[...].astype(F32)
    wown[0:1, 0:PER] = wraw[...].astype(F32)
    kappa = jnp.broadcast_to(kap[0:1], (BS, 128))
    st0[0:1] = jnp.broadcast_to(jnp.sum(wown[0:1], axis=1, keepdims=True), (1, 128))

    for part in range(LOADS):
        loads[part].wait()

        @pl.loop(part * (BS // LOADS), (part + 1) * (BS // LOADS))
        def _(x):
            for y in range(BS):
                cp[x + 1, y + 1, Z0:Z1, 0:PER] = raw[0, x, y]

    for part in range(LOADS):
        loads[LOADS + part].wait()

        @pl.loop(part * (BS // LOADS), (part + 1) * (BS // LOADS))
        def _(x):
            for y in range(BS):
                sf[x, y, :, 0:PER] = raw[1, x, y]


    copies = []

    def send(src, dst, send_sem, recv_sem, peer):
        copy = pltpu.make_async_remote_copy(
            src_ref=src, dst_ref=dst, send_sem=send_sem, recv_sem=recv_sem,
            device_id=(peer,), device_id_type=MESH,
        )
        copy.start()
        copies.append(copy)
        return copy

    def near(kind, d, slot):
        name, *at = kind
        if name == "face":
            step, pair = at
            faces = pl.ds(2 * pair, 2)
            return spk.at[step, d, faces], rpk.at[step, slot, faces], face_send.at[step, d, pair], face_recv.at[step, slot, pair]
        if name == "weights":
            row = pl.ds(0, 1)
            return wown.at[row], wnear.at[slot, row], w_send.at[d], w_recv.at[slot]
        (chunk,) = at
        sems = move_send.at[d, chunk], move_recv.at[slot, chunk]
        if chunk < INNER_CHUNKS:
            planes = pl.ds(INNER_CUTS[chunk], INNER_CUTS[chunk + 1] - INNER_CUTS[chunk])
            return spk_in.at[d, planes], rpk_in.at[slot, planes], *sems
        if chunk == INNER_CHUNKS:
            return spk_mid.at[d], rpk_mid.at[slot], *sems
        planes = pl.ds(2 * (chunk - INNER_CHUNKS - 1), 2)
        return spk_out.at[d, planes], rpk_out.at[slot, planes], *sems

    kinds = [("face", step, pair) for step in range(2) for pair in range(3)]
    kinds += [("weights",)] + [("move", chunk) for chunk in range(CHUNKS)]

    def send_sides(kind):
        for d, (peer, slot) in enumerate(sides):
            send(*near(kind, d, slot), peer)

    def take(kind, slot):
        src, place, send_sem, recv_sem = near(kind, 0, slot)
        pltpu.make_async_copy(place, place, recv_sem).wait()

    def take_sides(kind):
        take(kind, 0)
        take(kind, 1)

    def send_sums(stage):
        buf = stage_bufs[stage]
        base = sum(size - 1 for _, size in STAGES[:stage]) - 1
        return [
            send(buf.at[pl.ds(0, 1)], buf.at[pl.ds(j, 1)], sum_send.at[base + j], sum_recv.at[base + j], partner(stage, j))
            for j in range(1, STAGES[stage][1])
        ]

    def take_sums(stage, arrivals):
        for copy in arrivals:
            copy.wait_recv()
        stride, size = STAGES[stage]
        digit = lax.rem(me // stride, size)
        row = lax.broadcasted_iota(jnp.int32, (8, 128), 0)
        values = stage_bufs[stage][...]
        before = jnp.sum(jnp.where((row >= 1) & (row <= digit), values, 0.0), axis=0, keepdims=True)
        whole = jnp.sum(jnp.where(row < size, values, 0.0), axis=0, keepdims=True)
        return before, whole

    def own(f, layer, a):
        if f >= 4:
            return ftz[f - 4, layer, a]
        depth = 1 if layer == 1 else 0
        at = depth if f % 2 == 0 else BS - 1 - depth
        if f < 2:
            return sf[at, a] if layer == 2 else cp[1 + at, 1 + a, Z0:Z1]
        return sf[a, at] if layer == 2 else cp[1 + a, 1 + at, Z0:Z1]

    def draw_z():
        for a in range(BS):
            ftz[0, 0, a] = cp[1 + a, 1 : BS + 1, Z0]
            ftz[0, 1, a] = cp[1 + a, 1 : BS + 1, Z0 + 1]
            ftz[0, 2, a] = sf[a, :, 0]
            ftz[1, 0, a] = cp[1 + a, 1 : BS + 1, Z1 - 1]
            ftz[1, 1, a] = cp[1 + a, 1 : BS + 1, Z1 - 2]
            ftz[1, 2, a] = sf[a, :, BS - 1]

    def pack_pair(step, pair):
        for f in (2 * pair, 2 * pair + 1):
            for layer in range(3):
                rows = [own(f, layer, a) for a in range(BS)]
                turned = [pltpu.roll(rows[a], 16 * (a // 2), axis=1) if a >= 2 else rows[a] for a in range(BS)]
                to_left, to_right = turned[0:2], turned[0:2]
                for j in range(1, 8):
                    to_left = [jnp.where(slot16 == j, turned[2 * j + aa], to_left[aa]) for aa in range(2)]
                    to_right = [jnp.where(slot16 == (j + 3) % 8, turned[2 * j + aa], to_right[aa]) for aa in range(2)]
                to_left = [pltpu.roll(rows, 64, axis=1) for rows in to_left]
                to_right = [pltpu.roll(rows, 64, axis=1) for rows in to_right]
                for a in range(BS):
                    turned_own[f, layer, a] = turned[a]
                for aa in range(2):
                    spk[step, 0, f, layer, aa] = to_left[aa]
                    spk[step, 1, f, layer, aa] = to_right[aa]

    def ghost_face(step, f):
        g = f ^ 1
        place = jnp.broadcast_to(ints[f : f + 1], (BS, 128))
        inside = place >= 0
        place = place - me * PER
        for layer in range(3):
            from_right = [rpk[step, 0, g, layer, aa] for aa in range(2)]
            from_left = [rpk[step, 1, g, layer, aa] for aa in range(2)]
            table = []
            for a in range(BS):
                rows = jnp.where(slot16 == (a // 2 + 4) % 8, from_right[a % 2], turned_own[g, layer, a])
                table.append(jnp.where(slot16 == (a // 2 + 7) % 8, from_left[a % 2], rows))
            picked = [
                jnp.take_along_axis(table[a], jnp.bitwise_and(place + 16 * (a // 2), 127), axis=1, mode="promise_in_bounds")
                for a in range(BS)
            ]
            ghost = [jnp.where(inside, picked[a], own(f, layer, a)) for a in range(BS)]
            for a in range(BS):
                if layer == 0:
                    slab[f, a, Z0:Z1] = ghost[a]
                    slab[f, a, Z0 - 1 : Z0] = ghost[a][0:1]
                    slab[f, a, Z1 : Z1 + 1] = ghost[a][BS - 1 : BS]
                else:
                    slab2[f, layer - 1, a] = ghost[a]
        done = []
        for a in range(BS):
            g1 = slab[f, a, Z0:Z1]
            g2 = slab2[f, 0, a]
            gs = slab2[f, 1, a]
            around = slab[f, max(a - 1, 0), Z0:Z1] + slab[f, min(a + 1, BS - 1), Z0:Z1]
            around = around + slab[f, a, Z0 - 1 : Z1 - 1] + slab[f, a, Z0 + 1 : Z1 + 1]
            lap = kappa * (g2 + own(f, 0, a) + around - 6.0 * g1)
            square = g1 * g1
            mu = g1 * square - g1 - lap - 0.5 * gs
            excess = gs - 0.5 * square
            done.append((mu, excess, kappa * g1))
        for a in range(BS):
            mu, excess, part = done[a]
            if f < 2:
                edge = 0 if f == 0 else BS + 1
                cell = 1 if f == 0 else BS
                mp[edge, 1 + a, Z0:Z1] = mu
                ep[edge, 1 + a, Z0:Z1] = excess
                mp[cell, 1 + a, Z0:Z1] = mp[cell, 1 + a, Z0:Z1] - part
            elif f < 4:
                edge = 0 if f == 2 else BS + 1
                cell = 1 if f == 2 else BS
                mp[1 + a, edge, Z0:Z1] = mu
                ep[1 + a, edge, Z0:Z1] = excess
                mp[1 + a, cell, Z0:Z1] = mp[1 + a, cell, Z0:Z1] - part
            else:
                edge = Z0 - 1 if f == 4 else Z1
                cell = Z0 if f == 4 else Z1 - 1
                mp[1 + a, 1 : BS + 1, edge] = mu
                ep[1 + a, 1 : BS + 1, edge] = excess
                mp[1 + a, 1 : BS + 1, cell] = mp[1 + a, 1 : BS + 1, cell] - part

    def around_of(ref, x, y):
        total = ref[x, y + 1, Z0:Z1] + ref[x + 2, y + 1, Z0:Z1]
        total = total + ref[x + 1, y, Z0:Z1] + ref[x + 1, y + 2, Z0:Z1]
        return total + ref[x + 1, y + 1, Z0 - 1 : Z1 - 1] + ref[x + 1, y + 1, Z0 + 1 : Z1 + 1]

    def potentials():
        bias = 6.0 * kappa - 1.0

        @pl.loop(0, BS)
        def _(x):
            for y in range(BS):
                c = cp[x + 1, y + 1, Z0:Z1]
                s = sf[x, y]
                square = c * c
                mp[x + 1, y + 1, Z0:Z1] = c * (square + bias) - kappa * around_of(cp, x, y) - 0.5 * s
                ep[x + 1, y + 1, Z0:Z1] = s - 0.5 * square

    c_rate = MOBILITY_STEP * kappa
    s_rate = DIFFUSE_STEP * kappa

    def next_c(x, y):
        return cp[x + 1, y + 1, Z0:Z1] + c_rate * (around_of(mp, x, y) - 6.0 * mp[x + 1, y + 1, Z0:Z1])

    def next_s(x, y):
        return sf[x, y] + s_rate * (around_of(ep, x, y) - 6.0 * ep[x + 1, y + 1, Z0:Z1])

    def send_faces(step):
        send_sides(("face", step, 2))
        for pair in (0, 1):
            pack_pair(step, pair)
            send_sides(("face", step, pair))

    def take_faces(step, pair):
        take_sides(("face", step, pair))
        ghost_face(step, 2 * pair)
        ghost_face(step, 2 * pair + 1)

    def renew(x, ys):
        for y in ys:
            cp[x + 1, y + 1, Z0:Z1] = next_c(x, y)
            sf[x, y] = next_s(x, y)

    draw_z()
    pack_pair(0, 2)
    pl.semaphore_wait(barrier, PARTNERS + 2 + spare.astype(jnp.int32) - (first | last).astype(jnp.int32))
    send_faces(0)
    send_sides(("weights",))
    potentials()
    sums0 = send_sums(0)

    for end, slot in ((first, 1), (last, 0)):

        @pl.when(end)
        def _(slot=slot):
            for kind in kinds:
                _, place, _, sem = near(kind, 0, slot)
                pltpu.make_async_copy(near(kind, 0, 2)[1], place, sem).start()

    take_faces(0, 2)

    @pl.loop(*INNER)
    def _(x):
        renew(x, range(*INNER))

    take_faces(0, 0)
    take_faces(0, 1)

    @pl.loop(*INNER)
    def _(x):
        renew(x, RIM)

    for x in RIM:
        renew(x, range(BS))

    draw_z()
    pack_pair(1, 2)
    send_faces(1)
    potentials()
    before, whole = take_sums(0, sums0)
    st1[0:1] = whole
    sums1 = send_sums(1)
    take_faces(1, 2)

    turns = (0, 64, 32, 96)

    def quad(yy):
        return RIM if yy == 3 else tuple(2 + yy + 3 * j for j in range(4))

    def evolve(x, groups, packed, plane):
        for comp, update in ((0, next_c), (1, next_s)):
            for some in (groups[:2], groups[2:]):
                quads = [[update(x, y) for y in quad(yy)] for yy in some]
                turned = [[pltpu.roll(q[j], turns[j], axis=1) if turns[j] else q[j] for j in range(4)] for q in quads]
                shown = [[turned[i][2] if j == 2 else pltpu.roll(q[j], 32, axis=1) for j in range(4)] for i, q in enumerate(quads)]
                for i, yy in enumerate(some):
                    u0, u1, u2, u3 = turned[i]
                    row = groups.index(yy)
                    packed[0, plane, comp, row] = jnp.where(slot32 == 0, u0, jnp.where(slot32 == 2, u1, jnp.where(slot32 == 1, u2, u3)))
                    packed[1, plane, comp, row] = jnp.where(slot32 == 1, u0, jnp.where(slot32 == 3, u1, jnp.where(slot32 == 2, u2, u3)))
                    for j, y in enumerate(quad(yy)):
                        out[comp, x, y] = shown[i][j]

    for chunk in range(INNER_CHUNKS):

        @pl.loop(INNER_CUTS[chunk], INNER_CUTS[chunk + 1])
        def _(plane):
            evolve(plane + 2, (0, 1, 2), spk_in, plane)

        send_sides(("move", chunk))

    before1, whole = take_sums(1, sums1)
    st2[0:1] = whole
    sums2 = send_sums(2)
    before = before + before1
    take_faces(1, 0)
    take_faces(1, 1)

    @pl.loop(0, 12)
    def _(plane):
        evolve(plane + 2, (3,), spk_mid, plane)

    send_sides(("move", INNER_CHUNKS))
    for part in range(2):
        for k in (2 * part, 2 * part + 1):
            evolve(RIM[k], (0, 1, 2, 3), spk_out, k)
        send_sides(("move", INNER_CHUNKS + 1 + part))

    before2, total = take_sums(2, sums2)
    before = before + before2
    take_sides(("weights",))
    lane1 = lax.broadcasted_iota(jnp.int32, (8, 128), 1)
    ours = jnp.broadcast_to(wown[0:1], (8, 128))
    lefts = jnp.broadcast_to(wnear[1, 0:1], (8, 128))
    rights = jnp.broadcast_to(wnear[0, 0:1], (8, 128))
    block = me * PER - 32 + lane1
    exists = (block >= 0) & (block < count * PER)
    window = jnp.where(
        (lane1 >= 32) & (lane1 < 96),
        pltpu.roll(ours, 32, axis=1),
        pltpu.roll(jnp.where(lane1 < 32, rights, lefts), 96, axis=1),
    )
    window = jnp.where(exists, window, 0.0)
    earlier = (lax.broadcasted_iota(jnp.int32, (128, 128), 0) < lax.broadcasted_iota(jnp.int32, (128, 128), 1)).astype(F32)
    upto = jnp.dot(window, earlier, preferred_element_type=F32)
    lead = jnp.sum(jnp.where(lane1 < 32, window, 0.0), axis=1, keepdims=True)
    prior = (jnp.broadcast_to(before, (8, 128)) - lead + upto).astype(jnp.int32) * count
    whole_sum = jnp.broadcast_to(total, (8, 128)).astype(jnp.int32)
    live8 = (prior >= me * whole_sum) & (prior < (me + 1) * whole_sum)
    live8 = live8 & exists
    live = jnp.broadcast_to(live8.astype(F32)[0:1], (BS, 128)) > 0.5

    odd = jnp.bitwise_and(slot32, 1) == 1
    middle = (lane >= 32) & (lane < 96)

    def settle(x, groups, packed, plane):
        for comp in range(2):
            from_right = [packed[0, plane, comp, row] for row in range(len(groups))]
            from_left = [packed[1, plane, comp, row] for row in range(len(groups))]
            even_rows = [jnp.where(odd, a, b) for a, b in zip(from_left, from_right)]
            odd_rows = [jnp.where(odd, b, a) for a, b in zip(from_left, from_right)]
            halos = [
                [pltpu.roll(rows, 96, axis=1) for rows in even_rows],
                [pltpu.roll(rows, 32, axis=1) for rows in even_rows],
                [pltpu.roll(rows, 64, axis=1) for rows in odd_rows],
                odd_rows,
            ]
            merged = [
                (y, jnp.where(live, jnp.where(middle, out[comp, x, y], halos[j][row]), 0.0))
                for row, yy in enumerate(groups)
                for j, y in enumerate(quad(yy))
            ]
            for y, value in merged:
                out[comp, x, y] = value

    for chunk in range(INNER_CHUNKS):
        take_sides(("move", chunk))

        @pl.loop(INNER_CUTS[chunk], INNER_CUTS[chunk + 1])
        def _(plane):
            settle(plane + 2, (0, 1, 2), rpk_in, plane)

    take_sides(("move", INNER_CHUNKS))

    @pl.loop(0, 12)
    def _(plane):
        settle(plane + 2, (3,), rpk_mid, plane)

    for part in range(2):
        take_sides(("move", INNER_CHUNKS + 1 + part))
        for k in (2 * part, 2 * part + 1):
            settle(RIM[k], (0, 1, 2, 3), rpk_out, k)

    for copy in copies:
        copy.wait_send()

    @pl.when(spare)
    def _():
        for kind in kinds:
            take(kind, 2)


def store_kernel(window, out, sems):
    parts = 4
    copies = [
        pltpu.make_async_copy(
            window.at[k // 2, pl.ds((k % 2) * 8, 8)], out.at[k // 2, pl.ds((k % 2) * 8, 8)], sems.at[k]
        )
        for k in range(parts)
    ]
    for copy in copies:
        copy.start()
    for copy in copies:
        copy.wait()


def body(fields, weights, levels, neighbours):
    v = pltpu.VMEM
    dma = pltpu.SemaphoreType.DMA
    hbm = pl.BlockSpec(memory_space=pltpu.HBM)
    fields, weights, levels, neighbours = (
        pltpu.with_memory_space_constraint(x, pltpu.HBM)
        for x in (fields, weights.reshape(1, PER), levels.reshape(1, PER), neighbours)
    )
    window = pl.pallas_call(
        kernel,
        out_shape=pltpu.VMEM((2, BS, BS, BS, 2 * PER), F32),
        in_specs=[hbm] * 4,
        out_specs=pl.BlockSpec(memory_space=pltpu.VMEM),
        scratch_shapes=[
            v((2, BS, BS, BS, PER), F32),
            v((1, PER), jnp.int32),
            v((1, PER), jnp.int32),
            v((6, PER), jnp.int32),
            v((BS + 2, BS + 2, 32, 128), F32),
            v((BS + 2, BS + 2, 32, 128), F32),
            v((BS + 2, BS + 2, 32, 128), F32),
            v((BS, BS, BS, 128), F32),
            v((2, 3, BS, BS, 128), F32),
            v((6, 3, BS, BS, 128), F32),
            v((6, BS, 32, 128), F32),
            v((6, 2, BS, BS, 128), F32),
            v((8, 128), jnp.int32),
            v((8, 128), F32),
            v((8, 128), F32),
            v((3, 8, 128), F32),
            v((8, 128), F32),
            v((8, 128), F32),
            v((8, 128), F32),
            v((2, 2, 6, 3, 2, BS, 128), F32),
            v((2, 3, 6, 3, 2, BS, 128), F32),
            v((2, 12, 2, 3, BS, 128), F32),
            v((3, 12, 2, 3, BS, 128), F32),
            v((2, 12, 2, 1, BS, 128), F32),
            v((3, 12, 2, 1, BS, 128), F32),
            v((2, 4, 2, 4, BS, 128), F32),
            v((3, 4, 2, 4, BS, 128), F32),
            dma((3 + 2 * LOADS,)),
            dma((2, 2, 3)),
            dma((2, 3, 3)),
            dma((2, CHUNKS)),
            dma((3, CHUNKS)),
            dma((PARTNERS,)),
            dma((PARTNERS,)),
            dma((2,)),
            dma((3,)),
        ],
        compiler_params=pltpu.CompilerParams(
            collective_id=0, has_side_effects=True, vmem_limit_bytes=44 << 20
        ),
        cost_estimate=pl.CostEstimate(flops=40_000_000, bytes_accessed=8 << 20, transcendentals=0),
    )(fields, weights, levels, neighbours)
    return pl.pallas_call(
        store_kernel,
        out_shape=jax.ShapeDtypeStruct((2, BS, BS, BS, 2 * PER), F32),
        in_specs=[pl.BlockSpec(memory_space=pltpu.VMEM)],
        out_specs=pl.BlockSpec(memory_space=pltpu.HBM),
        scratch_shapes=[dma((4,))],
        compiler_params=pltpu.CompilerParams(vmem_limit_bytes=8 << 20),
    )(pltpu.with_memory_space_constraint(window, pltpu.VMEM))


def solution(mesh):
    in_specs = (P(None, None, None, None, "curve"), P("curve"), P("curve"), P(None, "curve"))
    out_specs = P(None, None, None, None, "curve")
    return jax.shard_map(body, mesh=mesh, in_specs=in_specs, out_specs=out_specs, check_vma=False)
```

```python
import jax
import jax.numpy as jnp
from jax import lax
from jax.experimental import pallas as pl
from jax.experimental.pallas import tpu as pltpu
from jax.sharding import PartitionSpec as P

MOBILITY_STEP = 0.0006
DIFFUSE_STEP = 0.01
BS = 16
PER = 64
STAGES = ((1, 8), (8, 4), (32, 4))
PARTNERS = sum(size - 1 for _, size in STAGES)
LOADS = 2
RIM = (0, 1, BS - 2, BS - 1)
INNER = (2, BS - 2)
INNER_CUTS = (0, 1, 4, 8, 12)
INNER_CHUNKS = len(INNER_CUTS) - 1
CHUNKS = INNER_CHUNKS + 4
Z0 = 8
Z1 = Z0 + BS
MESH = pl.DeviceIdType.MESH
F32 = jnp.float32


def kernel(
    fields, weights, levels, nbrs, out,
    raw, wraw, lraw, nraw,
    cp, mp, ep, sf, ftz, turned_own, slab, slab2, ints, kap, wown, wnear, st0, st1, st2,
    spk, rpk, spk_in, rpk_in, spk_rim, rpk_rim, spk_mid, rpk_mid, spk_out, rpk_out,
    in_sem, face_send, face_recv, move_send, move_recv, sum_send, sum_recv, w_send, w_recv,
):
    me = lax.axis_index("curve")
    count = lax.axis_size("curve")
    first = me == 0
    last = me == count - 1
    left = jnp.where(first, 1, me - 1)
    right = jnp.where(last, count - 2, me + 1)
    spare = (me == 1) | (me == count - 2)
    sides = ((left, jnp.where(first, 2, 0)), (right, jnp.where(last, 2, 1)))
    stage_bufs = (st0, st1, st2)

    def partner(stage, j):
        stride, size = STAGES[stage]
        digit = lax.rem(me // stride, size)
        return me + (lax.rem(digit + j, size) - digit) * stride

    small = [
        pltpu.make_async_copy(weights, wraw, in_sem.at[0]),
        pltpu.make_async_copy(levels, lraw, in_sem.at[1]),
        pltpu.make_async_copy(nbrs, nraw, in_sem.at[2]),
    ]
    loads = []
    for comp in range(2):
        for part in range(LOADS):
            planes = pl.ds(part * (BS // LOADS), BS // LOADS)
            loads.append(pltpu.make_async_copy(fields.at[comp, planes], raw.at[comp, planes], in_sem.at[3 + comp * LOADS + part]))
    for load in small + loads:
        load.start()

    barrier = pltpu.get_barrier_semaphore()
    for peer in (left, right):
        pl.semaphore_signal(barrier, inc=1, device_id=(peer,), device_id_type=MESH)
    for stage, (_, size) in enumerate(STAGES):
        for j in range(1, size):
            pl.semaphore_signal(barrier, inc=1, device_id=(partner(stage, j),), device_id_type=MESH)

    lane = lax.broadcasted_iota(jnp.int32, (BS, 128), 1)
    slot16 = lane // 16
    slot32 = lane // 32

    blank = jnp.zeros((BS, 128), F32)
    for a in range(BS):
        cp[0, 1 + a, Z0:Z1] = blank
        cp[BS + 1, 1 + a, Z0:Z1] = blank
        cp[1 + a, 0, Z0:Z1] = blank
        cp[1 + a, BS + 1, Z0:Z1] = blank
        cp[1 + a, 1 : BS + 1, Z0 - 1] = blank
        cp[1 + a, 1 : BS + 1, Z1] = blank

    ints[...] = jnp.zeros((8, 128), jnp.int32)
    kap[...] = jnp.zeros((8, 128), F32)
    wown[...] = jnp.zeros((8, 128), F32)
    for load in small:
        load.wait()
    ints[0:6, 0:PER] = nraw[...]
    kap[0:1, 0:PER] = 1.0 + 3.0 * lraw[...].astype(F32)
    wown[0:1, 0:PER] = wraw[...].astype(F32)
    kappa = jnp.broadcast_to(kap[0:1], (BS, 128))
    st0[0:1] = jnp.broadcast_to(jnp.sum(wown[0:1], axis=1, keepdims=True), (1, 128))

    for part in range(LOADS):
        loads[part].wait()

        @pl.loop(part * (BS // LOADS), (part + 1) * (BS // LOADS))
        def _(x):
            for y in range(BS):
                cp[x + 1, y + 1, Z0:Z1, 0:PER] = raw[0, x, y]

    for part in range(LOADS):
        loads[LOADS + part].wait()

        @pl.loop(part * (BS // LOADS), (part + 1) * (BS // LOADS))
        def _(x):
            for y in range(BS):
                sf[x, y, :, 0:PER] = raw[1, x, y]


    copies = []

    def send(src, dst, send_sem, recv_sem, peer):
        copy = pltpu.make_async_remote_copy(
            src_ref=src, dst_ref=dst, send_sem=send_sem, recv_sem=recv_sem,
            device_id=(peer,), device_id_type=MESH,
        )
        copy.start()
        copies.append(copy)
        return copy

    def near(kind, d, slot):
        name, *at = kind
        if name == "face":
            step, pair = at
            faces = pl.ds(2 * pair, 2)
            return spk.at[step, d, faces], rpk.at[step, slot, faces], face_send.at[step, d, pair], face_recv.at[step, slot, pair]
        if name == "weights":
            row = pl.ds(0, 1)
            return wown.at[row], wnear.at[slot, row], w_send.at[d], w_recv.at[slot]
        (chunk,) = at
        sems = move_send.at[d, chunk], move_recv.at[slot, chunk]
        if chunk < INNER_CHUNKS:
            planes = pl.ds(INNER_CUTS[chunk], INNER_CUTS[chunk + 1] - INNER_CUTS[chunk])
            cut = planes, slice(None), slice(None), pl.ds(2, 12)
            return spk_in.at[d, *cut], rpk_in.at[slot, *cut], *sems
        if chunk == INNER_CHUNKS:
            return spk_rim.at[d], rpk_rim.at[slot], *sems
        if chunk == INNER_CHUNKS + 1:
            return spk_mid.at[d], rpk_mid.at[slot], *sems
        planes = pl.ds(2 * (chunk - INNER_CHUNKS - 2), 2)
        return spk_out.at[d, planes], rpk_out.at[slot, planes], *sems

    kinds = [("face", step, pair) for step in range(2) for pair in range(3)]
    kinds += [("weights",)] + [("move", chunk) for chunk in range(CHUNKS)]

    def send_sides(kind):
        for d, (peer, slot) in enumerate(sides):
            send(*near(kind, d, slot), peer)

    def take(kind, slot):
        src, place, send_sem, recv_sem = near(kind, 0, slot)
        pltpu.make_async_copy(place, place, recv_sem).wait()

    def take_sides(kind):
        take(kind, 0)
        take(kind, 1)

    def send_sums(stage):
        buf = stage_bufs[stage]
        base = sum(size - 1 for _, size in STAGES[:stage]) - 1
        return [
            send(buf.at[pl.ds(0, 1)], buf.at[pl.ds(j, 1)], sum_send.at[base + j], sum_recv.at[base + j], partner(stage, j))
            for j in range(1, STAGES[stage][1])
        ]

    def take_sums(stage, arrivals):
        for copy in arrivals:
            copy.wait_recv()
        stride, size = STAGES[stage]
        digit = lax.rem(me // stride, size)
        row = lax.broadcasted_iota(jnp.int32, (8, 128), 0)
        values = stage_bufs[stage][...]
        before = jnp.sum(jnp.where((row >= 1) & (row <= digit), values, 0.0), axis=0, keepdims=True)
        whole = jnp.sum(jnp.where(row < size, values, 0.0), axis=0, keepdims=True)
        return before, whole

    def own(f, layer, a):
        if f >= 4:
            return ftz[f - 4, layer, a]
        depth = 1 if layer == 1 else 0
        at = depth if f % 2 == 0 else BS - 1 - depth
        if f < 2:
            return sf[at, a] if layer == 2 else cp[1 + at, 1 + a, Z0:Z1]
        return sf[a, at] if layer == 2 else cp[1 + a, 1 + at, Z0:Z1]

    def draw_z():
        for a in range(BS):
            ftz[0, 0, a] = cp[1 + a, 1 : BS + 1, Z0]
            ftz[0, 1, a] = cp[1 + a, 1 : BS + 1, Z0 + 1]
            ftz[0, 2, a] = sf[a, :, 0]
            ftz[1, 0, a] = cp[1 + a, 1 : BS + 1, Z1 - 1]
            ftz[1, 1, a] = cp[1 + a, 1 : BS + 1, Z1 - 2]
            ftz[1, 2, a] = sf[a, :, BS - 1]

    def pack_pair(step, pair):
        for f in (2 * pair, 2 * pair + 1):
            for layer in range(3):
                rows = [own(f, layer, a) for a in range(BS)]
                turned = [pltpu.roll(rows[a], 16 * (a // 2), axis=1) if a >= 2 else rows[a] for a in range(BS)]
                to_left, to_right = turned[0:2], turned[0:2]
                for j in range(1, 8):
                    to_left = [jnp.where(slot16 == j, turned[2 * j + aa], to_left[aa]) for aa in range(2)]
                    to_right = [jnp.where(slot16 == (j + 3) % 8, turned[2 * j + aa], to_right[aa]) for aa in range(2)]
                to_left = [pltpu.roll(rows, 64, axis=1) for rows in to_left]
                to_right = [pltpu.roll(rows, 64, axis=1) for rows in to_right]
                for a in range(BS):
                    turned_own[f, layer, a] = turned[a]
                for aa in range(2):
                    spk[step, 0, f, layer, aa] = to_left[aa]
                    spk[step, 1, f, layer, aa] = to_right[aa]

    def ghost_face(step, f):
        g = f ^ 1
        place = jnp.broadcast_to(ints[f : f + 1], (BS, 128))
        inside = place >= 0
        place = place - me * PER
        for layer in range(3):
            from_right = [rpk[step, 0, g, layer, aa] for aa in range(2)]
            from_left = [rpk[step, 1, g, layer, aa] for aa in range(2)]
            table = []
            for a in range(BS):
                rows = jnp.where(slot16 == (a // 2 + 4) % 8, from_right[a % 2], turned_own[g, layer, a])
                table.append(jnp.where(slot16 == (a // 2 + 7) % 8, from_left[a % 2], rows))
            picked = [
                jnp.take_along_axis(table[a], jnp.bitwise_and(place + 16 * (a // 2), 127), axis=1, mode="promise_in_bounds")
                for a in range(BS)
            ]
            ghost = [jnp.where(inside, picked[a], own(f, layer, a)) for a in range(BS)]
            for a in range(BS):
                if layer == 0:
                    slab[f, a, Z0:Z1] = ghost[a]
                    slab[f, a, Z0 - 1 : Z0] = ghost[a][0:1]
                    slab[f, a, Z1 : Z1 + 1] = ghost[a][BS - 1 : BS]
                else:
                    slab2[f, layer - 1, a] = ghost[a]
        done = []
        for a in range(BS):
            g1 = slab[f, a, Z0:Z1]
            g2 = slab2[f, 0, a]
            gs = slab2[f, 1, a]
            around = slab[f, max(a - 1, 0), Z0:Z1] + slab[f, min(a + 1, BS - 1), Z0:Z1]
            around = around + slab[f, a, Z0 - 1 : Z1 - 1] + slab[f, a, Z0 + 1 : Z1 + 1]
            lap = kappa * (g2 + own(f, 0, a) + around - 6.0 * g1)
            square = g1 * g1
            mu = g1 * square - g1 - lap - 0.5 * gs
            excess = gs - 0.5 * square
            done.append((mu, excess, kappa * g1))
        for a in range(BS):
            mu, excess, part = done[a]
            if f < 2:
                edge = 0 if f == 0 else BS + 1
                cell = 1 if f == 0 else BS
                mp[edge, 1 + a, Z0:Z1] = mu
                ep[edge, 1 + a, Z0:Z1] = excess
                mp[cell, 1 + a, Z0:Z1] = mp[cell, 1 + a, Z0:Z1] - part
            elif f < 4:
                edge = 0 if f == 2 else BS + 1
                cell = 1 if f == 2 else BS
                mp[1 + a, edge, Z0:Z1] = mu
                ep[1 + a, edge, Z0:Z1] = excess
                mp[1 + a, cell, Z0:Z1] = mp[1 + a, cell, Z0:Z1] - part
            else:
                edge = Z0 - 1 if f == 4 else Z1
                cell = Z0 if f == 4 else Z1 - 1
                mp[1 + a, 1 : BS + 1, edge] = mu
                ep[1 + a, 1 : BS + 1, edge] = excess
                mp[1 + a, 1 : BS + 1, cell] = mp[1 + a, 1 : BS + 1, cell] - part

    def around_of(ref, x, y):
        total = ref[x, y + 1, Z0:Z1] + ref[x + 2, y + 1, Z0:Z1]
        total = total + ref[x + 1, y, Z0:Z1] + ref[x + 1, y + 2, Z0:Z1]
        return total + ref[x + 1, y + 1, Z0 - 1 : Z1 - 1] + ref[x + 1, y + 1, Z0 + 1 : Z1 + 1]

    def potentials():
        bias = 6.0 * kappa - 1.0

        @pl.loop(0, BS)
        def _(x):
            for y in range(BS):
                c = cp[x + 1, y + 1, Z0:Z1]
                s = sf[x, y]
                square = c * c
                mp[x + 1, y + 1, Z0:Z1] = c * (square + bias) - kappa * around_of(cp, x, y) - 0.5 * s
                ep[x + 1, y + 1, Z0:Z1] = s - 0.5 * square

    c_rate = MOBILITY_STEP * kappa
    s_rate = DIFFUSE_STEP * kappa

    def next_c(x, y):
        return cp[x + 1, y + 1, Z0:Z1] + c_rate * (around_of(mp, x, y) - 6.0 * mp[x + 1, y + 1, Z0:Z1])

    def next_s(x, y):
        return sf[x, y] + s_rate * (around_of(ep, x, y) - 6.0 * ep[x + 1, y + 1, Z0:Z1])

    def send_faces(step):
        send_sides(("face", step, 2))
        for pair in (0, 1):
            pack_pair(step, pair)
            send_sides(("face", step, pair))

    def take_faces(step, pair):
        take_sides(("face", step, pair))
        ghost_face(step, 2 * pair)
        ghost_face(step, 2 * pair + 1)

    def renew(x, ys):
        for y in ys:
            cp[x + 1, y + 1, Z0:Z1] = next_c(x, y)
            sf[x, y] = next_s(x, y)

    draw_z()
    pack_pair(0, 2)
    pl.semaphore_wait(barrier, PARTNERS + 2 + spare.astype(jnp.int32) - (first | last).astype(jnp.int32))
    send_faces(0)
    send_sides(("weights",))
    potentials()
    sums0 = send_sums(0)

    for end, slot in ((first, 1), (last, 0)):

        @pl.when(end)
        def _(slot=slot):
            for kind in kinds:
                _, place, _, sem = near(kind, 0, slot)
                pltpu.make_async_copy(near(kind, 0, 2)[1], place, sem).start()

    take_faces(0, 2)

    @pl.loop(*INNER)
    def _(x):
        renew(x, range(*INNER))

    take_faces(0, 0)
    take_faces(0, 1)

    @pl.loop(1, BS // 2 - 1)
    def _(k):
        renew(2 * k, RIM)
        renew(2 * k + 1, RIM)

    for x in RIM:
        renew(x, range(BS))

    draw_z()
    pack_pair(1, 2)
    send_faces(1)
    potentials()

    turns = (0, 64, 32, 96)

    def quad(yy):
        return RIM if yy == 3 else tuple(2 + yy + 3 * j for j in range(4))

    def evolve(x, groups, packed, plane, ends=False):
        for comp, update in ((0, next_c), (1, next_s)):
            for some in (groups[:2], groups[2:]):
                quads = [[update(x, y) for y in quad(yy)] for yy in some]
                turned = [[pltpu.roll(q[j], turns[j], axis=1) if turns[j] else q[j] for j in range(4)] for q in quads]
                shown = [[turned[i][2] if j == 2 else pltpu.roll(q[j], 32, axis=1) for j in range(4)] for i, q in enumerate(quads)]
                for i, yy in enumerate(some):
                    u0, u1, u2, u3 = turned[i]
                    row = groups.index(yy)
                    to_left = jnp.where(slot32 == 0, u0, jnp.where(slot32 == 2, u1, jnp.where(slot32 == 1, u2, u3)))
                    to_right = jnp.where(slot32 == 1, u0, jnp.where(slot32 == 3, u1, jnp.where(slot32 == 2, u2, u3)))
                    for d, rows in ((0, to_left), (1, to_right)):
                        if ends:
                            packed[d, plane, row, 4 * comp : 4 * comp + 2] = rows[0:2]
                            packed[d, plane, row, 4 * comp + 2 : 4 * comp + 4] = rows[BS - 2 : BS]
                        else:
                            packed[d, plane, comp, row] = rows
                    for j, y in enumerate(quad(yy)):
                        out[comp, x, y] = shown[i][j]

    for chunk in range(INNER_CHUNKS):

        @pl.loop(INNER_CUTS[chunk], INNER_CUTS[chunk + 1])
        def _(plane):
            evolve(plane + 2, (0, 1, 2), spk_in, plane)

        send_sides(("move", chunk))

    before, whole = take_sums(0, sums0)
    st1[0:1] = whole
    sums1 = send_sums(1)
    take_faces(1, 2)

    @pl.loop(0, 12)
    def _(plane):
        evolve(plane + 2, (0, 1, 2), spk_rim, plane, ends=True)

    send_sides(("move", INNER_CHUNKS))
    before1, whole = take_sums(1, sums1)
    st2[0:1] = whole
    sums2 = send_sums(2)
    before = before + before1
    take_faces(1, 0)
    take_faces(1, 1)

    @pl.loop(0, 6)
    def _(k):
        evolve(2 * k + 2, (3,), spk_mid, 2 * k)
        evolve(2 * k + 3, (3,), spk_mid, 2 * k + 1)

    send_sides(("move", INNER_CHUNKS + 1))
    for part in range(2):
        for k in (2 * part, 2 * part + 1):
            evolve(RIM[k], (0, 1, 2, 3), spk_out, k)
        send_sides(("move", INNER_CHUNKS + 2 + part))

    before2, total = take_sums(2, sums2)
    before = before + before2
    take_sides(("weights",))
    lane1 = lax.broadcasted_iota(jnp.int32, (8, 128), 1)
    ours = jnp.broadcast_to(wown[0:1], (8, 128))
    lefts = jnp.broadcast_to(wnear[1, 0:1], (8, 128))
    rights = jnp.broadcast_to(wnear[0, 0:1], (8, 128))
    block = me * PER - 32 + lane1
    exists = (block >= 0) & (block < count * PER)
    window = jnp.where(
        (lane1 >= 32) & (lane1 < 96),
        pltpu.roll(ours, 32, axis=1),
        pltpu.roll(jnp.where(lane1 < 32, rights, lefts), 96, axis=1),
    )
    window = jnp.where(exists, window, 0.0)
    earlier = (lax.broadcasted_iota(jnp.int32, (128, 128), 0) < lax.broadcasted_iota(jnp.int32, (128, 128), 1)).astype(F32)
    upto = jnp.dot(window, earlier, preferred_element_type=F32)
    lead = jnp.sum(jnp.where(lane1 < 32, window, 0.0), axis=1, keepdims=True)
    prior = (jnp.broadcast_to(before, (8, 128)) - lead + upto).astype(jnp.int32) * count
    whole_sum = jnp.broadcast_to(total, (8, 128)).astype(jnp.int32)
    live8 = (prior >= me * whole_sum) & (prior < (me + 1) * whole_sum)
    live8 = live8 & exists
    live = jnp.broadcast_to(live8.astype(F32)[0:1], (BS, 128)) > 0.5

    odd = jnp.bitwise_and(slot32, 1) == 1
    middle = (lane >= 32) & (lane < 96)

    def settle(x, groups, packed, plane):
        for comp in range(2):
            from_right = [packed[0, plane, comp, row] for row in range(len(groups))]
            from_left = [packed[1, plane, comp, row] for row in range(len(groups))]
            even_rows = [jnp.where(odd, a, b) for a, b in zip(from_left, from_right)]
            odd_rows = [jnp.where(odd, b, a) for a, b in zip(from_left, from_right)]
            halos = [
                [pltpu.roll(rows, 96, axis=1) for rows in even_rows],
                [pltpu.roll(rows, 32, axis=1) for rows in even_rows],
                [pltpu.roll(rows, 64, axis=1) for rows in odd_rows],
                odd_rows,
            ]
            merged = [
                (y, jnp.where(live, jnp.where(middle, out[comp, x, y], halos[j][row]), 0.0))
                for row, yy in enumerate(groups)
                for j, y in enumerate(quad(yy))
            ]
            for y, value in merged:
                out[comp, x, y] = value

    for chunk in range(INNER_CHUNKS + 1):
        take_sides(("move", chunk))

    @pl.loop(0, 12)
    def _(plane):
        for slot in range(2):
            for comp in range(2):
                for row in range(3):
                    rpk_in[slot, plane, comp, row, 0:2] = rpk_rim[slot, plane, row, 4 * comp : 4 * comp + 2]
                    rpk_in[slot, plane, comp, row, BS - 2 : BS] = rpk_rim[slot, plane, row, 4 * comp + 2 : 4 * comp + 4]
        settle(plane + 2, (0, 1, 2), rpk_in, plane)

    take_sides(("move", INNER_CHUNKS + 1))

    @pl.loop(0, 6)
    def _(k):
        settle(2 * k + 2, (3,), rpk_mid, 2 * k)
        settle(2 * k + 3, (3,), rpk_mid, 2 * k + 1)

    for part in range(2):
        take_sides(("move", INNER_CHUNKS + 2 + part))
        for k in (2 * part, 2 * part + 1):
            settle(RIM[k], (0, 1, 2, 3), rpk_out, k)

    for copy in copies:
        copy.wait_send()

    @pl.when(spare)
    def _():
        for kind in kinds:
            take(kind, 2)


def store_kernel(window, out, sems):
    parts = 4
    copies = [
        pltpu.make_async_copy(
            window.at[k // 2, pl.ds((k % 2) * 8, 8)], out.at[k // 2, pl.ds((k % 2) * 8, 8)], sems.at[k]
        )
        for k in range(parts)
    ]
    for copy in copies:
        copy.start()
    for copy in copies:
        copy.wait()


def body(fields, weights, levels, neighbours):
    v = pltpu.VMEM
    dma = pltpu.SemaphoreType.DMA
    hbm = pl.BlockSpec(memory_space=pltpu.HBM)
    fields, weights, levels, neighbours = (
        pltpu.with_memory_space_constraint(x, pltpu.HBM)
        for x in (fields, weights.reshape(1, PER), levels.reshape(1, PER), neighbours)
    )
    window = pl.pallas_call(
        kernel,
        out_shape=pltpu.VMEM((2, BS, BS, BS, 2 * PER), F32),
        in_specs=[hbm] * 4,
        out_specs=pl.BlockSpec(memory_space=pltpu.VMEM),
        scratch_shapes=[
            v((2, BS, BS, BS, PER), F32),
            v((1, PER), jnp.int32),
            v((1, PER), jnp.int32),
            v((6, PER), jnp.int32),
            v((BS + 2, BS + 2, 32, 128), F32),
            v((BS + 2, BS + 2, 32, 128), F32),
            v((BS + 2, BS + 2, 32, 128), F32),
            v((BS, BS, BS, 128), F32),
            v((2, 3, BS, BS, 128), F32),
            v((6, 3, BS, BS, 128), F32),
            v((6, BS, 32, 128), F32),
            v((6, 2, BS, BS, 128), F32),
            v((8, 128), jnp.int32),
            v((8, 128), F32),
            v((8, 128), F32),
            v((3, 8, 128), F32),
            v((8, 128), F32),
            v((8, 128), F32),
            v((8, 128), F32),
            v((2, 2, 6, 3, 2, BS, 128), F32),
            v((2, 3, 6, 3, 2, BS, 128), F32),
            v((2, 12, 2, 3, BS, 128), F32),
            v((3, 12, 2, 3, BS, 128), F32),
            v((2, 12, 3, 8, 128), F32),
            v((3, 12, 3, 8, 128), F32),
            v((2, 12, 2, 1, BS, 128), F32),
            v((3, 12, 2, 1, BS, 128), F32),
            v((2, 4, 2, 4, BS, 128), F32),
            v((3, 4, 2, 4, BS, 128), F32),
            dma((3 + 2 * LOADS,)),
            dma((2, 2, 3)),
            dma((2, 3, 3)),
            dma((2, CHUNKS)),
            dma((3, CHUNKS)),
            dma((PARTNERS,)),
            dma((PARTNERS,)),
            dma((2,)),
            dma((3,)),
        ],
        compiler_params=pltpu.CompilerParams(
            collective_id=0, has_side_effects=True, vmem_limit_bytes=44 << 20
        ),
        cost_estimate=pl.CostEstimate(flops=40_000_000, bytes_accessed=8 << 20, transcendentals=0),
    )(fields, weights, levels, neighbours)
    return pl.pallas_call(
        store_kernel,
        out_shape=jax.ShapeDtypeStruct((2, BS, BS, BS, 2 * PER), F32),
        in_specs=[pl.BlockSpec(memory_space=pltpu.VMEM)],
        out_specs=pl.BlockSpec(memory_space=pltpu.HBM),
        scratch_shapes=[dma((4,))],
        compiler_params=pltpu.CompilerParams(vmem_limit_bytes=8 << 20),
    )(pltpu.with_memory_space_constraint(window, pltpu.VMEM))


def solution(mesh):
    in_specs = (P(None, None, None, None, "curve"), P("curve"), P("curve"), P(None, "curve"))
    out_specs = P(None, None, None, None, "curve")
    return jax.shard_map(body, mesh=mesh, in_specs=in_specs, out_specs=out_specs, check_vma=False)
```

```python
import jax
import jax.numpy as jnp
from jax import lax
from jax.experimental import pallas as pl
from jax.experimental.pallas import tpu as pltpu
from jax.sharding import PartitionSpec as P

MOBILITY_STEP = 0.0006
DIFFUSE_STEP = 0.01
BS = 16
PER = 64
STAGES = ((1, 8), (8, 4), (32, 4))
PARTNERS = sum(size - 1 for _, size in STAGES)
LOADS = 2
RIM = (0, 1, BS - 2, BS - 1)
INNER = (2, BS - 2)
INNER_CUTS = (0, 1, 4, 8, 12)
INNER_CHUNKS = len(INNER_CUTS) - 1
CHUNKS = INNER_CHUNKS + 4
Z0 = 8
Z1 = Z0 + BS
MESH = pl.DeviceIdType.MESH
F32 = jnp.float32


def kernel(
    fields, weights, levels, nbrs, out,
    raw, wraw, lraw, nraw,
    cp, mp, ep, sf, ftz, turned_own, slab, slab2, ints, kap, wown, wnear, st0, st1, st2,
    spk, rpk, spk_in, rpk_in, spk_rim, rpk_rim, spk_mid, rpk_mid, spk_out, rpk_out,
    in_sem, face_send, face_recv, move_send, move_recv, sum_send, sum_recv, w_send, w_recv,
):
    me = lax.axis_index("curve")
    count = lax.axis_size("curve")
    first = me == 0
    last = me == count - 1
    left = jnp.where(first, 1, me - 1)
    right = jnp.where(last, count - 2, me + 1)
    spare = (me == 1) | (me == count - 2)
    sides = ((left, jnp.where(first, 2, 0)), (right, jnp.where(last, 2, 1)))
    stage_bufs = (st0, st1, st2)

    def partner(stage, j):
        stride, size = STAGES[stage]
        digit = lax.rem(me // stride, size)
        return me + (lax.rem(digit + j, size) - digit) * stride

    small = [
        pltpu.make_async_copy(weights, wraw, in_sem.at[0]),
        pltpu.make_async_copy(levels, lraw, in_sem.at[1]),
        pltpu.make_async_copy(nbrs, nraw, in_sem.at[2]),
    ]
    loads = []
    for comp in range(2):
        for part in range(LOADS):
            planes = pl.ds(part * (BS // LOADS), BS // LOADS)
            loads.append(pltpu.make_async_copy(fields.at[comp, planes], raw.at[comp, planes], in_sem.at[3 + comp * LOADS + part]))
    for load in small + loads:
        load.start()

    barrier = pltpu.get_barrier_semaphore()
    for peer in (left, right):
        pl.semaphore_signal(barrier, inc=1, device_id=(peer,), device_id_type=MESH)
    for stage, (_, size) in enumerate(STAGES):
        for j in range(1, size):
            pl.semaphore_signal(barrier, inc=1, device_id=(partner(stage, j),), device_id_type=MESH)

    lane = lax.broadcasted_iota(jnp.int32, (BS, 128), 1)
    slot16 = lane // 16
    slot32 = lane // 32

    blank = jnp.zeros((BS, 128), F32)
    for a in range(BS):
        cp[0, 1 + a, Z0:Z1] = blank
        cp[BS + 1, 1 + a, Z0:Z1] = blank
        cp[1 + a, 0, Z0:Z1] = blank
        cp[1 + a, BS + 1, Z0:Z1] = blank
        cp[1 + a, 1 : BS + 1, Z0 - 1] = blank
        cp[1 + a, 1 : BS + 1, Z1] = blank

    ints[...] = jnp.zeros((8, 128), jnp.int32)
    kap[...] = jnp.zeros((8, 128), F32)
    wown[...] = jnp.zeros((8, 128), F32)
    for load in small:
        load.wait()
    ints[0:6, 0:PER] = nraw[...]
    kap[0:1, 0:PER] = 1.0 + 3.0 * lraw[...].astype(F32)
    wown[0:1, 0:PER] = wraw[...].astype(F32)
    kappa = jnp.broadcast_to(kap[0:1], (BS, 128))
    st0[0:1] = jnp.broadcast_to(jnp.sum(wown[0:1], axis=1, keepdims=True), (1, 128))

    for part in range(LOADS):
        loads[part].wait()

        @pl.loop(part * (BS // LOADS), (part + 1) * (BS // LOADS))
        def _(x):
            for y in range(BS):
                cp[x + 1, y + 1, Z0:Z1, 0:PER] = raw[0, x, y]

    for part in range(LOADS):
        loads[LOADS + part].wait()

        @pl.loop(part * (BS // LOADS), (part + 1) * (BS // LOADS))
        def _(x):
            for y in range(BS):
                sf[x, y, :, 0:PER] = raw[1, x, y]


    copies = []

    def send(src, dst, send_sem, recv_sem, peer):
        copy = pltpu.make_async_remote_copy(
            src_ref=src, dst_ref=dst, send_sem=send_sem, recv_sem=recv_sem,
            device_id=(peer,), device_id_type=MESH,
        )
        copy.start()
        copies.append(copy)
        return copy

    def near(kind, d, slot):
        name, *at = kind
        if name == "face":
            step, pair = at
            faces = pl.ds(2 * pair, 2)
            return spk.at[step, d, faces], rpk.at[step, slot, faces], face_send.at[step, d, pair], face_recv.at[step, slot, pair]
        if name == "weights":
            row = pl.ds(0, 1)
            return wown.at[row], wnear.at[slot, row], w_send.at[d], w_recv.at[slot]
        (chunk,) = at
        sems = move_send.at[d, chunk], move_recv.at[slot, chunk]
        if chunk < INNER_CHUNKS:
            planes = pl.ds(INNER_CUTS[chunk], INNER_CUTS[chunk + 1] - INNER_CUTS[chunk])
            cut = planes, slice(None), slice(None), pl.ds(2, 12)
            return spk_in.at[d, *cut], rpk_in.at[slot, *cut], *sems
        if chunk == INNER_CHUNKS:
            return spk_rim.at[d], rpk_rim.at[slot], *sems
        if chunk == INNER_CHUNKS + 1:
            return spk_mid.at[d], rpk_mid.at[slot], *sems
        planes = pl.ds(2 * (chunk - INNER_CHUNKS - 2), 2)
        return spk_out.at[d, planes], rpk_out.at[slot, planes], *sems

    kinds = [("face", step, pair) for step in range(2) for pair in range(3)]
    kinds += [("weights",)] + [("move", chunk) for chunk in range(CHUNKS)]

    def send_sides(kind):
        for d, (peer, slot) in enumerate(sides):
            send(*near(kind, d, slot), peer)

    def take(kind, slot):
        src, place, send_sem, recv_sem = near(kind, 0, slot)
        pltpu.make_async_copy(place, place, recv_sem).wait()

    def take_sides(kind):
        take(kind, 0)
        take(kind, 1)

    def send_sums(stage):
        buf = stage_bufs[stage]
        base = sum(size - 1 for _, size in STAGES[:stage]) - 1
        return [
            send(buf.at[pl.ds(0, 1)], buf.at[pl.ds(j, 1)], sum_send.at[base + j], sum_recv.at[base + j], partner(stage, j))
            for j in range(1, STAGES[stage][1])
        ]

    def take_sums(stage, arrivals):
        for copy in arrivals:
            copy.wait_recv()
        stride, size = STAGES[stage]
        digit = lax.rem(me // stride, size)
        row = lax.broadcasted_iota(jnp.int32, (8, 128), 0)
        values = stage_bufs[stage][...]
        before = jnp.sum(jnp.where((row >= 1) & (row <= digit), values, 0.0), axis=0, keepdims=True)
        whole = jnp.sum(jnp.where(row < size, values, 0.0), axis=0, keepdims=True)
        return before, whole

    def own(f, layer, a):
        if f >= 4:
            return ftz[f - 4, layer, a]
        depth = 1 if layer == 1 else 0
        at = depth if f % 2 == 0 else BS - 1 - depth
        if f < 2:
            return sf[at, a] if layer == 2 else cp[1 + at, 1 + a, Z0:Z1]
        return sf[a, at] if layer == 2 else cp[1 + a, 1 + at, Z0:Z1]

    def draw_z():
        for a in range(BS):
            ftz[0, 0, a] = cp[1 + a, 1 : BS + 1, Z0]
            ftz[0, 1, a] = cp[1 + a, 1 : BS + 1, Z0 + 1]
            ftz[0, 2, a] = sf[a, :, 0]
            ftz[1, 0, a] = cp[1 + a, 1 : BS + 1, Z1 - 1]
            ftz[1, 1, a] = cp[1 + a, 1 : BS + 1, Z1 - 2]
            ftz[1, 2, a] = sf[a, :, BS - 1]

    def pack_pair(step, pair):
        for f in (2 * pair, 2 * pair + 1):
            for layer in range(3):
                rows = [own(f, layer, a) for a in range(BS)]
                turned = [pltpu.roll(rows[a], 16 * (a // 2), axis=1) if a >= 2 else rows[a] for a in range(BS)]
                to_left, to_right = turned[0:2], turned[0:2]
                for j in range(1, 8):
                    to_left = [jnp.where(slot16 == j, turned[2 * j + aa], to_left[aa]) for aa in range(2)]
                    to_right = [jnp.where(slot16 == (j + 3) % 8, turned[2 * j + aa], to_right[aa]) for aa in range(2)]
                to_left = [pltpu.roll(rows, 64, axis=1) for rows in to_left]
                to_right = [pltpu.roll(rows, 64, axis=1) for rows in to_right]
                for a in range(BS):
                    turned_own[f, layer, a] = turned[a]
                for aa in range(2):
                    spk[step, 0, f, layer, aa] = to_left[aa]
                    spk[step, 1, f, layer, aa] = to_right[aa]

    def ghost_face(step, f):
        g = f ^ 1
        place = jnp.broadcast_to(ints[f : f + 1], (BS, 128))
        inside = place >= 0
        place = place - me * PER
        for layer in range(3):
            from_right = [rpk[step, 0, g, layer, aa] for aa in range(2)]
            from_left = [rpk[step, 1, g, layer, aa] for aa in range(2)]
            table = []
            for a in range(BS):
                rows = jnp.where(slot16 == (a // 2 + 4) % 8, from_right[a % 2], turned_own[g, layer, a])
                table.append(jnp.where(slot16 == (a // 2 + 7) % 8, from_left[a % 2], rows))
            picked = [
                jnp.take_along_axis(table[a], jnp.bitwise_and(place + 16 * (a // 2), 127), axis=1, mode="promise_in_bounds")
                for a in range(BS)
            ]
            ghost = [jnp.where(inside, picked[a], own(f, layer, a)) for a in range(BS)]
            for a in range(BS):
                if layer == 0:
                    slab[f, a, Z0:Z1] = ghost[a]
                    slab[f, a, Z0 - 1 : Z0] = ghost[a][0:1]
                    slab[f, a, Z1 : Z1 + 1] = ghost[a][BS - 1 : BS]
                else:
                    slab2[f, layer - 1, a] = ghost[a]
        done = []
        for a in range(BS):
            g1 = slab[f, a, Z0:Z1]
            g2 = slab2[f, 0, a]
            gs = slab2[f, 1, a]
            around = slab[f, max(a - 1, 0), Z0:Z1] + slab[f, min(a + 1, BS - 1), Z0:Z1]
            around = around + slab[f, a, Z0 - 1 : Z1 - 1] + slab[f, a, Z0 + 1 : Z1 + 1]
            lap = kappa * (g2 + own(f, 0, a) + around - 6.0 * g1)
            square = g1 * g1
            mu = g1 * square - g1 - lap - 0.5 * gs
            excess = gs - 0.5 * square
            done.append((mu, excess, kappa * g1))
        for a in range(BS):
            mu, excess, part = done[a]
            if f < 2:
                edge = 0 if f == 0 else BS + 1
                cell = 1 if f == 0 else BS
                mp[edge, 1 + a, Z0:Z1] = mu
                ep[edge, 1 + a, Z0:Z1] = excess
                mp[cell, 1 + a, Z0:Z1] = mp[cell, 1 + a, Z0:Z1] - part
            elif f < 4:
                edge = 0 if f == 2 else BS + 1
                cell = 1 if f == 2 else BS
                mp[1 + a, edge, Z0:Z1] = mu
                ep[1 + a, edge, Z0:Z1] = excess
                mp[1 + a, cell, Z0:Z1] = mp[1 + a, cell, Z0:Z1] - part
            else:
                edge = Z0 - 1 if f == 4 else Z1
                cell = Z0 if f == 4 else Z1 - 1
                mp[1 + a, 1 : BS + 1, edge] = mu
                ep[1 + a, 1 : BS + 1, edge] = excess
                mp[1 + a, 1 : BS + 1, cell] = mp[1 + a, 1 : BS + 1, cell] - part

    def around_of(ref, x, y):
        total = ref[x, y + 1, Z0:Z1] + ref[x + 2, y + 1, Z0:Z1]
        total = total + ref[x + 1, y, Z0:Z1] + ref[x + 1, y + 2, Z0:Z1]
        return total + ref[x + 1, y + 1, Z0 - 1 : Z1 - 1] + ref[x + 1, y + 1, Z0 + 1 : Z1 + 1]

    def potentials():
        bias = 6.0 * kappa - 1.0

        @pl.loop(0, BS)
        def _(x):
            for y in range(BS):
                c = cp[x + 1, y + 1, Z0:Z1]
                s = sf[x, y]
                square = c * c
                mp[x + 1, y + 1, Z0:Z1] = c * (square + bias) - kappa * around_of(cp, x, y) - 0.5 * s
                ep[x + 1, y + 1, Z0:Z1] = s - 0.5 * square

    c_rate = MOBILITY_STEP * kappa
    s_rate = DIFFUSE_STEP * kappa

    def next_c(x, y):
        return cp[x + 1, y + 1, Z0:Z1] + c_rate * (around_of(mp, x, y) - 6.0 * mp[x + 1, y + 1, Z0:Z1])

    def next_s(x, y):
        return sf[x, y] + s_rate * (around_of(ep, x, y) - 6.0 * ep[x + 1, y + 1, Z0:Z1])

    def take_faces(step, pair):
        take_sides(("face", step, pair))
        ghost_face(step, 2 * pair)
        ghost_face(step, 2 * pair + 1)

    def renew(x, ys):
        for y in ys:
            cp[x + 1, y + 1, Z0:Z1] = next_c(x, y)
            sf[x, y] = next_s(x, y)

    draw_z()
    pack_pair(0, 2)
    pl.semaphore_wait(barrier, PARTNERS + 2 + spare.astype(jnp.int32) - (first | last).astype(jnp.int32))
    send_sides(("face", 0, 2))
    for pair in (0, 1):
        pack_pair(0, pair)
        send_sides(("face", 0, pair))
    send_sides(("weights",))
    potentials()
    sums0 = send_sums(0)

    for end, slot in ((first, 1), (last, 0)):

        @pl.when(end)
        def _(slot=slot):
            for kind in kinds:
                _, place, _, sem = near(kind, 0, slot)
                pltpu.make_async_copy(near(kind, 0, 2)[1], place, sem).start()

    take_faces(0, 2)

    @pl.loop(*INNER)
    def _(x):
        renew(x, range(*INNER))

    take_faces(0, 0)
    take_faces(0, 1)

    for x in RIM:
        renew(x, range(BS))

    pack_pair(1, 0)
    send_sides(("face", 1, 0))

    @pl.loop(1, BS // 2 - 1)
    def _(k):
        renew(2 * k, RIM)
        renew(2 * k + 1, RIM)

    draw_z()
    for pair in (2, 1):
        pack_pair(1, pair)
        send_sides(("face", 1, pair))

    potentials()

    turns = (0, 64, 32, 96)

    def quad(yy):
        return RIM if yy == 3 else tuple(2 + yy + 3 * j for j in range(4))

    def evolve(x, groups, packed, plane, ends=False):
        for comp, update in ((0, next_c), (1, next_s)):
            for some in (groups[:2], groups[2:]):
                quads = [[update(x, y) for y in quad(yy)] for yy in some]
                turned = [[pltpu.roll(q[j], turns[j], axis=1) if turns[j] else q[j] for j in range(4)] for q in quads]
                shown = [[turned[i][2] if j == 2 else pltpu.roll(q[j], 32, axis=1) for j in range(4)] for i, q in enumerate(quads)]
                for i, yy in enumerate(some):
                    u0, u1, u2, u3 = turned[i]
                    row = groups.index(yy)
                    to_left = jnp.where(slot32 == 0, u0, jnp.where(slot32 == 2, u1, jnp.where(slot32 == 1, u2, u3)))
                    to_right = jnp.where(slot32 == 1, u0, jnp.where(slot32 == 3, u1, jnp.where(slot32 == 2, u2, u3)))
                    for d, rows in ((0, to_left), (1, to_right)):
                        if ends:
                            packed[d, plane, row, 4 * comp : 4 * comp + 2] = rows[0:2]
                            packed[d, plane, row, 4 * comp + 2 : 4 * comp + 4] = rows[BS - 2 : BS]
                        else:
                            packed[d, plane, comp, row] = rows
                    for j, y in enumerate(quad(yy)):
                        out[comp, x, y] = shown[i][j]

    for chunk in range(INNER_CHUNKS):

        @pl.loop(INNER_CUTS[chunk], INNER_CUTS[chunk + 1])
        def _(plane):
            evolve(plane + 2, (0, 1, 2), spk_in, plane)

        send_sides(("move", chunk))

    before, whole = take_sums(0, sums0)
    st1[0:1] = whole
    sums1 = send_sums(1)
    take_faces(1, 0)
    take_faces(1, 2)

    @pl.loop(0, 12)
    def _(plane):
        evolve(plane + 2, (0, 1, 2), spk_rim, plane, ends=True)

    send_sides(("move", INNER_CHUNKS))
    take_faces(1, 1)

    @pl.loop(0, 6)
    def _(k):
        evolve(2 * k + 2, (3,), spk_mid, 2 * k)
        evolve(2 * k + 3, (3,), spk_mid, 2 * k + 1)

    send_sides(("move", INNER_CHUNKS + 1))
    before1, whole = take_sums(1, sums1)
    st2[0:1] = whole
    sums2 = send_sums(2)
    before = before + before1
    for part in range(2):
        for k in (2 * part, 2 * part + 1):
            evolve(RIM[k], (0, 1, 2, 3), spk_out, k)
        send_sides(("move", INNER_CHUNKS + 2 + part))

    before2, total = take_sums(2, sums2)
    before = before + before2
    take_sides(("weights",))
    lane1 = lax.broadcasted_iota(jnp.int32, (8, 128), 1)
    ours = jnp.broadcast_to(wown[0:1], (8, 128))
    lefts = jnp.broadcast_to(wnear[1, 0:1], (8, 128))
    rights = jnp.broadcast_to(wnear[0, 0:1], (8, 128))
    block = me * PER - 32 + lane1
    exists = (block >= 0) & (block < count * PER)
    window = jnp.where(
        (lane1 >= 32) & (lane1 < 96),
        pltpu.roll(ours, 32, axis=1),
        pltpu.roll(jnp.where(lane1 < 32, rights, lefts), 96, axis=1),
    )
    window = jnp.where(exists, window, 0.0)
    earlier = (lax.broadcasted_iota(jnp.int32, (128, 128), 0) < lax.broadcasted_iota(jnp.int32, (128, 128), 1)).astype(F32)
    upto = jnp.dot(window, earlier, preferred_element_type=F32)
    lead = jnp.sum(jnp.where(lane1 < 32, window, 0.0), axis=1, keepdims=True)
    prior = (jnp.broadcast_to(before, (8, 128)) - lead + upto).astype(jnp.int32) * count
    whole_sum = jnp.broadcast_to(total, (8, 128)).astype(jnp.int32)
    live8 = (prior >= me * whole_sum) & (prior < (me + 1) * whole_sum)
    live8 = live8 & exists
    live = jnp.broadcast_to(live8.astype(F32)[0:1], (BS, 128)) > 0.5

    odd = jnp.bitwise_and(slot32, 1) == 1
    middle = (lane >= 32) & (lane < 96)

    def settle(x, groups, packed, plane):
        for comp in range(2):
            from_right = [packed[0, plane, comp, row] for row in range(len(groups))]
            from_left = [packed[1, plane, comp, row] for row in range(len(groups))]
            even_rows = [jnp.where(odd, a, b) for a, b in zip(from_left, from_right)]
            odd_rows = [jnp.where(odd, b, a) for a, b in zip(from_left, from_right)]
            halos = [
                [pltpu.roll(rows, 96, axis=1) for rows in even_rows],
                [pltpu.roll(rows, 32, axis=1) for rows in even_rows],
                [pltpu.roll(rows, 64, axis=1) for rows in odd_rows],
                odd_rows,
            ]
            merged = [
                (y, jnp.where(live, jnp.where(middle, out[comp, x, y], halos[j][row]), 0.0))
                for row, yy in enumerate(groups)
                for j, y in enumerate(quad(yy))
            ]
            for y, value in merged:
                out[comp, x, y] = value

    for chunk in range(INNER_CHUNKS + 1):
        take_sides(("move", chunk))

    @pl.loop(0, 12)
    def _(plane):
        for slot in range(2):
            for comp in range(2):
                for row in range(3):
                    rpk_in[slot, plane, comp, row, 0:2] = rpk_rim[slot, plane, row, 4 * comp : 4 * comp + 2]
                    rpk_in[slot, plane, comp, row, BS - 2 : BS] = rpk_rim[slot, plane, row, 4 * comp + 2 : 4 * comp + 4]
        settle(plane + 2, (0, 1, 2), rpk_in, plane)

    take_sides(("move", INNER_CHUNKS + 1))

    @pl.loop(0, 6)
    def _(k):
        settle(2 * k + 2, (3,), rpk_mid, 2 * k)
        settle(2 * k + 3, (3,), rpk_mid, 2 * k + 1)

    for part in range(2):
        take_sides(("move", INNER_CHUNKS + 2 + part))
        for k in (2 * part, 2 * part + 1):
            settle(RIM[k], (0, 1, 2, 3), rpk_out, k)

    for copy in copies:
        copy.wait_send()

    @pl.when(spare)
    def _():
        for kind in kinds:
            take(kind, 2)


def store_kernel(window, out, sems):
    parts = 4
    copies = [
        pltpu.make_async_copy(
            window.at[k // 2, pl.ds((k % 2) * 8, 8)], out.at[k // 2, pl.ds((k % 2) * 8, 8)], sems.at[k]
        )
        for k in range(parts)
    ]
    for copy in copies:
        copy.start()
    for copy in copies:
        copy.wait()


def body(fields, weights, levels, neighbours):
    v = pltpu.VMEM
    dma = pltpu.SemaphoreType.DMA
    hbm = pl.BlockSpec(memory_space=pltpu.HBM)
    fields, weights, levels, neighbours = (
        pltpu.with_memory_space_constraint(x, pltpu.HBM)
        for x in (fields, weights.reshape(1, PER), levels.reshape(1, PER), neighbours)
    )
    window = pl.pallas_call(
        kernel,
        out_shape=pltpu.VMEM((2, BS, BS, BS, 2 * PER), F32),
        in_specs=[hbm] * 4,
        out_specs=pl.BlockSpec(memory_space=pltpu.VMEM),
        scratch_shapes=[
            v((2, BS, BS, BS, PER), F32),
            v((1, PER), jnp.int32),
            v((1, PER), jnp.int32),
            v((6, PER), jnp.int32),
            v((BS + 2, BS + 2, 32, 128), F32),
            v((BS + 2, BS + 2, 32, 128), F32),
            v((BS + 2, BS + 2, 32, 128), F32),
            v((BS, BS, BS, 128), F32),
            v((2, 3, BS, BS, 128), F32),
            v((6, 3, BS, BS, 128), F32),
            v((6, BS, 32, 128), F32),
            v((6, 2, BS, BS, 128), F32),
            v((8, 128), jnp.int32),
            v((8, 128), F32),
            v((8, 128), F32),
            v((3, 8, 128), F32),
            v((8, 128), F32),
            v((8, 128), F32),
            v((8, 128), F32),
            v((2, 2, 6, 3, 2, BS, 128), F32),
            v((2, 3, 6, 3, 2, BS, 128), F32),
            v((2, 12, 2, 3, BS, 128), F32),
            v((3, 12, 2, 3, BS, 128), F32),
            v((2, 12, 3, 8, 128), F32),
            v((3, 12, 3, 8, 128), F32),
            v((2, 12, 2, 1, BS, 128), F32),
            v((3, 12, 2, 1, BS, 128), F32),
            v((2, 4, 2, 4, BS, 128), F32),
            v((3, 4, 2, 4, BS, 128), F32),
            dma((3 + 2 * LOADS,)),
            dma((2, 2, 3)),
            dma((2, 3, 3)),
            dma((2, CHUNKS)),
            dma((3, CHUNKS)),
            dma((PARTNERS,)),
            dma((PARTNERS,)),
            dma((2,)),
            dma((3,)),
        ],
        compiler_params=pltpu.CompilerParams(
            collective_id=0, has_side_effects=True, vmem_limit_bytes=44 << 20
        ),
        cost_estimate=pl.CostEstimate(flops=40_000_000, bytes_accessed=8 << 20, transcendentals=0),
    )(fields, weights, levels, neighbours)
    return pl.pallas_call(
        store_kernel,
        out_shape=jax.ShapeDtypeStruct((2, BS, BS, BS, 2 * PER), F32),
        in_specs=[pl.BlockSpec(memory_space=pltpu.VMEM)],
        out_specs=pl.BlockSpec(memory_space=pltpu.HBM),
        scratch_shapes=[dma((4,))],
        compiler_params=pltpu.CompilerParams(vmem_limit_bytes=8 << 20),
    )(pltpu.with_memory_space_constraint(window, pltpu.VMEM))


def solution(mesh):
    in_specs = (P(None, None, None, None, "curve"), P("curve"), P("curve"), P(None, "curve"))
    out_specs = P(None, None, None, None, "curve")
    return jax.shard_map(body, mesh=mesh, in_specs=in_specs, out_specs=out_specs, check_vma=False)
```
